512 devices in a mesh: gz: 64 (over z, y), gy: 8 (over x, core).
Axes of the slice: x: 4, y: 8, z: 8, core: 2. Of those that a mesh axis runs over, the one named last changes fastest.
Arguments:
- source: float32 [128, 512, 512], P('gz', 'gy'), may hold values from -6 to 6
- screening: float32 [128], replicated, may hold values from 1e-05 to 0.002
Outputs:
- pressure: float32 [128, 512, 512], P('gz', 'gy')
The draws below stay inside these ranges and needn't reach their ends.
All inputs are finite; a program needn't handle non-finite values.
Results may differ from the reference program's by a relative error of at most 0.00045.
Values sent between devices are 32-bit elements; how exact they have to be, the bound alone decides.
No kernel may reach another device: no remote copies, remote signals or barrier semaphores. Data moves between devices by JAX's collectives and lax.ppermute only.
A program may use at most 192 MiB of HBM per device.

```python
import math
import jax
import jax.numpy as jnp
from jax import lax

NX = 512
NY = 512
NZ = 128


def draw_source(key, part):
    key = jax.random.fold_in(key, 11)
    first = jax.random.fold_in(key, 0)
    values = jax.random.normal(first, (NZ, NY, NX), jnp.float32)
    return jnp.clip(values, -6.0, 6.0)


def setup_inputs(seed: int = 0) -> dict:
    seeds = jax.random.split(jax.random.key(seed), 3)
    source = draw_source(jax.random.fold_in(seeds[2], 71), 0)
    screening = jnp.clip(jnp.exp(jax.random.uniform(seeds[1], (NZ,), jnp.float32, math.log(9.999999747378752e-06), math.log(0.002))), 9.999999747378752e-06, 0.002)
    return {"source": source, "screening": screening}


def hartley(values, axis):
    spectrum = jnp.fft.fft(values, axis=axis)
    return (spectrum.real - spectrum.imag).astype(values.dtype)


def wave_term(total):
    index = jnp.arange(total, dtype=jnp.int32).astype(jnp.float32)
    return 2.0 - 2.0 * jnp.cos(index * (2.0 * math.pi / total))


def reference(source, screening):
    fourier_modes = hartley(hartley(source, 2), 1)
    lam = wave_term(NY)[:, None] + wave_term(NX)[None, :]
    zero_array = jnp.zeros((NY, NX), jnp.float32)

    def forward_sweep(loop_carry, current_row):
        previous_pivot, previous_elimination = loop_carry
        right_hand_side, shift = current_row
        pivot_entry = 1.0 / (2.0 + shift + lam - previous_pivot)
        elimination_factor = pivot_entry * (right_hand_side + previous_elimination)
        return (pivot_entry, elimination_factor), (pivot_entry, elimination_factor)

    unused_slot, (pivot_entries, elimination_factors) = lax.scan(forward_sweep, (zero_array, zero_array), (fourier_modes, screening))

    def backward_sweep(upper_diagonal, current_row):
        pivot_entry, elimination_factor = current_row
        row_value = elimination_factor + pivot_entry * upper_diagonal
        return row_value, row_value

    unused_slot, solved_rows = lax.scan(backward_sweep, zero_array, (pivot_entries, elimination_factors), reverse=True)
    return hartley(hartley(solved_rows, 1), 2) / (NX * NY)
```

```python
import math

import jax
import jax.numpy as jnp
import ml_dtypes
import numpy as np
from jax import lax
from jax.experimental import pallas as pl
from jax.experimental.pallas import tpu as pltpu
from jax.sharding import PartitionSpec as P

NX = 512
NY = 512
NZ = 128
HALF = 256
CHUNKS = 8
RUN = NZ // CHUNKS
LINES = 8
PEERS = 64

F32 = jnp.float32
BF16 = jnp.bfloat16


def split_table(table):
    high = table.astype(ml_dtypes.bfloat16)
    low = (table - high.astype(np.float64)).astype(ml_dtypes.bfloat16)
    return np.concatenate([high, low], axis=0)


def cas(rows, columns, total):
    angle = (rows[:, None] * columns[None, :] % total) * (2.0 * math.pi / total)
    return np.cos(angle) + np.sin(angle)


def half_tables():
    index = np.arange(HALF)
    even = cas(2 * index, index, 2 * HALF)
    odd = cas(2 * index + 1, index, 2 * HALF)
    return split_table(even), split_table(odd), split_table(odd.T)


def wave_terms():
    index = np.concatenate([np.arange(0, 512, 2), np.arange(1, 512, 2)])
    return (4.0 * np.sin(index * (math.pi / 512)) ** 2).astype(np.float32)


def split(values):
    high = values.astype(BF16)
    low = (values - high.astype(F32)).astype(BF16)
    return high, low


def times_table(values, table_ref):
    rows = values.shape[0]
    high, low = split(values)
    both = jnp.concatenate([high, low], axis=0)
    main = jnp.dot(both, table_ref[:HALF], preferred_element_type=F32)
    rest = jnp.dot(high, table_ref[HALF:], preferred_element_type=F32)
    return main[:rows] + (main[rows:] + rest)


def table_times_transposed(table_ref, values):
    rows = values.shape[0]
    high, low = split(values)
    both = jnp.concatenate([high, low], axis=0)
    product = lax.dot_general(
        table_ref[...], both, (((1,), (1,)), ((), ())), preferred_element_type=F32
    )
    return product[:HALF, :rows] + (product[:HALF, rows:] + product[HALF:, :rows])


def forward_x_kernel(source_ref, even_ref, odd_ref, out_ref):
    rows = source_ref[...].reshape(128, NX)
    low, high = rows[:, :HALF], rows[:, HALF:]
    out_ref[:HALF] = table_times_transposed(even_ref, low + high)
    out_ref[HALF:] = table_times_transposed(odd_ref, low - high)


def pivots_kernel(place_ref, screening_ref, wave_k_ref, wave_l_ref, pivot_ref, up_ref, down_ref, far_ref, close_ref, state_ref):
    chunk, group = place_ref[0], place_ref[1]
    line = lax.broadcasted_iota(jnp.int32, (LINES, NY), 0)
    lam = jnp.zeros((LINES, NY), F32) + wave_l_ref[...]
    for k in range(LINES):
        lam = lam + jnp.where(line == k, wave_k_ref[group * LINES + k], 0.0)
    one = jnp.ones((LINES, NY), F32)

    def step(plane, total, rise):
        rise = rise + (screening_ref[plane] + lam) * total
        return total + rise, rise

    def lap(index, state):
        below, above = state
        other = CHUNKS - 1 - index

        @pl.when(index == chunk)
        def _():
            state_ref[0] = below

        @pl.when(other == chunk)
        def _():
            state_ref[1] = above

        low_total, low_rise, high_total, high_rise = one, below, one, above
        for t in range(RUN):
            low_total, low_rise = step(index * RUN + t, low_total, low_rise)
            high_total, high_rise = step(other * RUN + RUN - 1 - t, high_total, high_rise)
        low_inverse, high_inverse = 1.0 / low_total, 1.0 / high_total

        @pl.when(index < chunk)
        def _():
            far_ref[index] = low_inverse

        @pl.when(other > chunk)
        def _():
            far_ref[other] = high_inverse

        return low_rise * low_inverse, high_rise * high_inverse

    far_ref[chunk] = jnp.zeros((LINES, NY), F32)
    lax.fori_loop(0, CHUNKS, lap, (one, one))

    first = chunk * RUN
    total, rise = one, state_ref[0]
    for t in range(RUN):
        up_ref[t] = total
        before = total
        total, rise = step(first + t, total, rise)
        pivot_ref[t] = before / total
    inverse = 1.0 / total
    last_pivot = pivot_ref[RUN - 1]
    close_ref[...] = 1.0 / (rise * inverse + last_pivot * state_ref[1])
    for t in range(RUN):
        up_ref[t] = up_ref[t] * inverse

    total, rise = one, state_ref[1]
    for t in reversed(range(RUN)):
        down_ref[t] = total
        total, rise = step(first + t, total, rise)
    inverse = 1.0 / total
    for t in range(RUN):
        down_ref[t] = down_ref[t] * inverse


def swap_halves(values):
    shape = values.shape
    return pltpu.roll(values.reshape(-1, 128), 64, 1).reshape(shape)


def lower_half(shape):
    return lax.broadcasted_iota(jnp.int32, shape, len(shape) - 1) < 64


def forward_y_kernel(place_ref, rows_ref, even_ref, odd_t_ref, up_ref, down_ref, modes_ref, send_ref):
    chunk = place_ref[0]
    blocks = rows_ref[...].reshape(8, 8, LINES, 128)
    keep = lower_half((8, LINES, 128))

    def gather(parts):
        columns = []
        for pair in range(2):
            a, b = parts[2 * pair], parts[2 * pair + 1]
            first = jnp.where(keep, a, swap_halves(b))
            second = jnp.where(keep, swap_halves(a), b)
            columns.append(jnp.stack([first, second], axis=1).reshape(128, 128))
        return jnp.concatenate(columns, axis=1)

    sums = gather([blocks[:, g] + blocks[:, g + 4] for g in range(4)])
    differences = gather([blocks[:, g] - blocks[:, g + 4] for g in range(4)])
    modes_ref[:, :, :HALF] = times_table(sums, even_ref).reshape(RUN, LINES, HALF)
    modes_ref[:, :, HALF:] = times_table(differences, odd_t_ref).reshape(RUN, LINES, HALF)

    upward = jnp.zeros((LINES, NY), F32)
    downward = jnp.zeros((LINES, NY), F32)
    for t in range(RUN):
        plane = modes_ref[t]
        upward = upward + up_ref[t] * plane
        downward = downward + down_ref[t] * plane
    for other in range(CHUNKS):
        send_ref[other] = jnp.where(other > chunk, upward, downward)


def solve_kernel(place_ref, modes_ref, arrived_ref, pivot_ref, far_ref, close_ref, even_ref, odd_ref, out_ref, solved_ref):
    chunk = place_ref[0]
    below = jnp.zeros((LINES, NY), F32)
    above = jnp.zeros((LINES, NY), F32)
    for other in range(CHUNKS):
        below = jnp.where(other < chunk, arrived_ref[other] + far_ref[other] * below, below)
        rest = CHUNKS - 1 - other
        above = jnp.where(rest > chunk, arrived_ref[rest] + far_ref[rest] * above, above)

    elimination = below
    for t in range(RUN):
        elimination = pivot_ref[t] * (modes_ref[t] + elimination)
        solved_ref[t] = elimination
    value = (elimination + pivot_ref[RUN - 1] * above) * close_ref[...]
    solved_ref[RUN - 1] = value
    for t in reversed(range(RUN - 1)):
        value = solved_ref[t] + pivot_ref[t] * value
        solved_ref[t] = value

    solved = solved_ref[...].reshape(128, NY)
    even = times_table(solved[:, :HALF], even_ref)
    odd = times_table(solved[:, HALF:], odd_ref)
    keep = lower_half((8, LINES, 128))
    for base, values in ((0, even + odd), (4, even - odd)):
        for pair in range(2):
            column = values[:, pair * 128 : pair * 128 + 128].reshape(8, 2, LINES, 128)
            a, b = column[:, 0], column[:, 1]
            out_ref[:, base + 2 * pair] = jnp.where(keep, a, swap_halves(b))
            out_ref[:, base + 2 * pair + 1] = jnp.where(keep, swap_halves(a), b)


def backward_x_kernel(rows_ref, even_ref, odd_ref, out_ref):
    values = rows_ref[...].T
    even = times_table(values[:, :HALF], even_ref)
    odd = times_table(values[:, HALF:], odd_ref)
    scale = 1.0 / (NX * NY)
    out_ref[:, :, :HALF] = ((even + odd) * scale).reshape(2, 64, HALF)
    out_ref[:, :, HALF:] = ((even - odd) * scale).reshape(2, 64, HALF)


VMEM = pl.BlockSpec(memory_space=pltpu.VMEM)
SMEM = pl.BlockSpec(memory_space=pltpu.SMEM)


def call(kernel, ins, outs, scratch=(), name=None):
    return pl.pallas_call(
        kernel,
        in_specs=ins,
        out_specs=jax.tree.map(lambda _: VMEM, outs),
        out_shape=outs,
        scratch_shapes=list(scratch),
        compiler_params=pltpu.CompilerParams(vmem_limit_bytes=16 * 1024 * 1024),
        name=name,
    )


def shape(*sizes):
    return jax.ShapeDtypeStruct(sizes, F32)


RUN_PEERS = [[run * PEERS + peer for peer in range(PEERS)] for run in range(CHUNKS)]
RUNS = [[run * 8 + y for run in range(CHUNKS)] for y in range(8)]


def exchange_peers(values):
    pieces = values.reshape(PEERS, LINES, 128)
    pieces = lax.all_to_all(
        pieces, ("gz", "gy"), 0, 0, tiled=True, axis_index_groups=RUN_PEERS
    )
    return pieces.reshape(512, 128)


def local(source, screening):
    even, odd, odd_t = (jnp.asarray(table) for table in half_tables())
    waves = wave_terms()
    gz, gy = lax.axis_index("gz"), lax.axis_index("gy")
    place = jnp.stack([gz // 8, (gz % 8) * 8 + gy]).astype(jnp.int32)

    along_x = call(forward_x_kernel, [VMEM] * 3, shape(512, 128), name="forward_x")(
        source, even, odd
    )
    columns = exchange_peers(along_x)
    planes = shape(RUN, LINES, NY)
    pivots, up, down, far, close = call(
        pivots_kernel,
        [SMEM, SMEM, SMEM, VMEM],
        (planes, planes, planes, shape(CHUNKS, LINES, NY), shape(LINES, NY)),
        [pltpu.VMEM((2, LINES, NY), F32)],
        name="pivots",
    )(place, screening, jnp.asarray(waves), jnp.asarray(waves)[None, :])
    modes, send = call(
        forward_y_kernel,
        [SMEM] + [VMEM] * 5,
        (planes, shape(CHUNKS, LINES, NY)),
        name="forward_y",
    )(place, columns, even, odd_t, up, down)
    arrived = lax.all_to_all(send, "gz", 0, 0, tiled=True, axis_index_groups=RUNS)
    back_y = call(
        solve_kernel,
        [SMEM] + [VMEM] * 7,
        shape(8, 8, LINES, 128),
        [pltpu.VMEM((RUN, LINES, NY), F32)],
        name="solve",
    )(place, modes, arrived, pivots, far, close, even, odd)
    rows = exchange_peers(back_y)
    return call(backward_x_kernel, [VMEM] * 3, shape(2, 64, NX), name="backward_x")(
        rows, even, odd
    )


def solution(mesh):
    in_specs = (P("gz", "gy", None), P())
    out_specs = P("gz", "gy", None)
    return jax.shard_map(local, mesh=mesh, in_specs=in_specs, out_specs=out_specs, check_vma=False)
```

```python
import math

import jax
import jax.numpy as jnp
import ml_dtypes
import numpy as np
from jax import lax
from jax.experimental import pallas as pl
from jax.experimental.pallas import tpu as pltpu
from jax.sharding import PartitionSpec as P

NX = 512
NY = 512
NZ = 128
HALF = 256
CHUNKS = 8
RUN = NZ // CHUNKS
LINES = 8
PEERS = 64
FIRST_RUN = 4
FIRST_Y = 4

F32 = jnp.float32
BF16 = jnp.bfloat16


def split_table(table):
    high = table.astype(ml_dtypes.bfloat16)
    low = (table - high.astype(np.float64)).astype(ml_dtypes.bfloat16)
    return np.concatenate([high, low], axis=0)


def cas(rows, columns, total):
    angle = (rows[:, None] * columns[None, :] % total) * (2.0 * math.pi / total)
    return np.cos(angle) + np.sin(angle)


def half_tables():
    index = np.arange(HALF)
    even = cas(2 * index, index, 2 * HALF)
    odd = cas(2 * index + 1, index, 2 * HALF)
    return split_table(even), split_table(odd), split_table(odd.T)


def wave_terms():
    index = np.concatenate([np.arange(0, 512, 2), np.arange(1, 512, 2)])
    return (4.0 * np.sin(index * (math.pi / 512)) ** 2).astype(np.float32)


def split(values):
    high = values.astype(BF16)
    low = (values - high.astype(F32)).astype(BF16)
    return high, low


def times_table(values, table_ref):
    rows = values.shape[0]
    high, low = split(values)
    both = jnp.concatenate([high, low], axis=0)
    main = jnp.dot(both, table_ref[:HALF], preferred_element_type=F32)
    rest = jnp.dot(high, table_ref[HALF:], preferred_element_type=F32)
    return main[:rows] + (main[rows:] + rest)


def table_times_transposed(table_ref, values):
    rows = values.shape[0]
    high, low = split(values)
    both = jnp.concatenate([high, low], axis=0)
    product = lax.dot_general(
        table_ref[...], both, (((1,), (1,)), ((), ())), preferred_element_type=F32
    )
    return product[:HALF, :rows] + (product[:HALF, rows:] + product[HALF:, :rows])


def row(plane):
    return (plane - 2 * FIRST_Y) % RUN


def place_of_run(run):
    return (run - FIRST_RUN) % CHUNKS


def forward_x_kernel(source_hbm, even_hbm, odd_hbm, out_ref, source_ref, even_ref, odd_ref, arrived):
    copies = [
        pltpu.make_async_copy(source_hbm, source_ref, arrived.at[0]),
        pltpu.make_async_copy(even_hbm, even_ref, arrived.at[1]),
        pltpu.make_async_copy(odd_hbm, odd_ref, arrived.at[2]),
    ]
    for copy in copies:
        copy.start()
    for copy in copies:
        copy.wait()
    rows = source_ref[...].reshape(128, NX)
    low, high = rows[:, :HALF], rows[:, HALF:]
    out_ref[:HALF] = table_times_transposed(even_ref, low + high)
    out_ref[HALF:] = table_times_transposed(odd_ref, low - high)


def pivots_kernel(place_ref, screening_ref, wave_k_ref, wave_l_ref, pivot_ref, up_ref, down_ref, far_ref, close_ref, state_ref):
    chunk, group = place_ref[0], place_ref[1]
    line = lax.broadcasted_iota(jnp.int32, (LINES, NY), 0)
    lam = jnp.zeros((LINES, NY), F32) + wave_l_ref[...]
    for k in range(LINES):
        lam = lam + jnp.where(line == k, wave_k_ref[group * LINES + k], 0.0)
    one = jnp.ones((LINES, NY), F32)

    def step(plane, total, rise):
        rise = rise + (screening_ref[plane] + lam) * total
        return total + rise, rise

    def lap(index, state):
        below, above = state
        other = CHUNKS - 1 - index

        @pl.when(index == chunk)
        def _():
            state_ref[0] = below

        @pl.when(other == chunk)
        def _():
            state_ref[1] = above

        low_total, low_rise, high_total, high_rise = one, below, one, above
        for t in range(RUN):
            low_total, low_rise = step(index * RUN + t, low_total, low_rise)
            high_total, high_rise = step(other * RUN + RUN - 1 - t, high_total, high_rise)
        low_inverse, high_inverse = 1.0 / low_total, 1.0 / high_total

        @pl.when(index < chunk)
        def _():
            far_ref[index] = low_inverse

        @pl.when(other > chunk)
        def _():
            far_ref[other] = high_inverse

        return low_rise * low_inverse, high_rise * high_inverse

    far_ref[chunk] = jnp.zeros((LINES, NY), F32)
    lax.fori_loop(0, CHUNKS, lap, (one, one))

    first = chunk * RUN
    total, rise = one, state_ref[0]
    for t in range(RUN):
        up_ref[t] = total
        before = total
        total, rise = step(first + t, total, rise)
        pivot_ref[t] = before / total
    inverse = 1.0 / total
    last_pivot = pivot_ref[RUN - 1]
    close_ref[...] = 1.0 / (rise * inverse + last_pivot * state_ref[1])
    for t in range(RUN):
        up_ref[t] = up_ref[t] * inverse

    total, rise = one, state_ref[1]
    for t in reversed(range(RUN)):
        down_ref[t] = total
        total, rise = step(first + t, total, rise)
    inverse = 1.0 / total
    for t in range(RUN):
        down_ref[t] = down_ref[t] * inverse


def swap_halves(values):
    shape = values.shape
    return pltpu.roll(values.reshape(-1, 128), 64, 1).reshape(shape)


def lower_half(shape):
    return lax.broadcasted_iota(jnp.int32, shape, len(shape) - 1) < 64


def forward_y_kernel(place_ref, rows_ref, even_ref, odd_t_ref, up_ref, down_ref, modes_ref, send_ref):
    chunk = place_ref[0]
    blocks = rows_ref[...].reshape(8, 8, LINES, 128)
    keep = lower_half((8, LINES, 128))

    def gather(parts):
        columns = []
        for pair in range(2):
            a, b = parts[2 * pair], parts[2 * pair + 1]
            first = jnp.where(keep, a, swap_halves(b))
            second = jnp.where(keep, swap_halves(a), b)
            columns.append(jnp.stack([first, second], axis=1).reshape(128, 128))
        return jnp.concatenate(columns, axis=1)

    sums = gather([blocks[:, g] + blocks[:, g + 4] for g in range(4)])
    differences = gather([blocks[:, g] - blocks[:, g + 4] for g in range(4)])
    modes_ref[:, :, :HALF] = times_table(sums, even_ref).reshape(RUN, LINES, HALF)
    modes_ref[:, :, HALF:] = times_table(differences, odd_t_ref).reshape(RUN, LINES, HALF)

    upward = jnp.zeros((LINES, NY), F32)
    downward = jnp.zeros((LINES, NY), F32)
    for t in range(RUN):
        plane = modes_ref[row(t)]
        upward = upward + up_ref[t] * plane
        downward = downward + down_ref[t] * plane
    for other in range(CHUNKS):
        send_ref[place_of_run(other)] = jnp.where(other > chunk, upward, downward)


def solve_kernel(place_ref, modes_ref, arrived_ref, pivot_ref, far_ref, close_ref, even_ref, odd_ref, out_ref, solved_ref):
    chunk = place_ref[0]
    below = jnp.zeros((LINES, NY), F32)
    above = jnp.zeros((LINES, NY), F32)
    for other in range(CHUNKS):
        below = jnp.where(other < chunk, arrived_ref[place_of_run(other)] + far_ref[other] * below, below)
        rest = CHUNKS - 1 - other
        above = jnp.where(rest > chunk, arrived_ref[place_of_run(rest)] + far_ref[rest] * above, above)

    elimination = below
    for t in range(RUN):
        elimination = pivot_ref[t] * (modes_ref[row(t)] + elimination)
        solved_ref[row(t)] = elimination
    value = (elimination + pivot_ref[RUN - 1] * above) * close_ref[...]
    solved_ref[row(RUN - 1)] = value
    for t in reversed(range(RUN - 1)):
        value = solved_ref[row(t)] + pivot_ref[t] * value
        solved_ref[row(t)] = value

    solved = solved_ref[...].reshape(128, NY)
    even = times_table(solved[:, :HALF], even_ref)
    odd = times_table(solved[:, HALF:], odd_ref)
    keep = lower_half((8, LINES, 128))
    for base, values in ((0, even + odd), (4, even - odd)):
        for pair in range(2):
            column = values[:, pair * 128 : pair * 128 + 128].reshape(8, 2, LINES, 128)
            a, b = column[:, 0], column[:, 1]
            out_ref[:, base + 2 * pair] = jnp.where(keep, a, swap_halves(b))
            out_ref[:, base + 2 * pair + 1] = jnp.where(keep, swap_halves(a), b)


def backward_x_kernel(rows_ref, even_ref, odd_ref, out_ref):
    values = rows_ref[...].T
    even = times_table(values[:, :HALF], even_ref)
    odd = times_table(values[:, HALF:], odd_ref)
    scale = 1.0 / (NX * NY)
    out_ref[:, :, :HALF] = ((even + odd) * scale).reshape(2, 64, HALF)
    out_ref[:, :, HALF:] = ((even - odd) * scale).reshape(2, 64, HALF)


VMEM = pl.BlockSpec(memory_space=pltpu.VMEM)
HBM = pl.BlockSpec(memory_space=pltpu.HBM)
SMEM = pl.BlockSpec(memory_space=pltpu.SMEM)


def call(kernel, ins, outs, scratch=(), name=None, limit=16 * 1024 * 1024):
    return pl.pallas_call(
        kernel,
        in_specs=ins,
        out_specs=jax.tree.map(lambda _: VMEM, outs),
        out_shape=outs,
        scratch_shapes=list(scratch),
        compiler_params=pltpu.CompilerParams(vmem_limit_bytes=limit),
        name=name,
    )


def shape(*sizes):
    return jax.ShapeDtypeStruct(sizes, F32)


RUN_PEERS = [
    [run * PEERS + (peer + FIRST_Y * 8) % PEERS for peer in range(PEERS)] for run in range(CHUNKS)
]
RUNS = [[(run + FIRST_RUN) % CHUNKS * 8 + y for run in range(CHUNKS)] for y in range(8)]


def exchange_peers(values):
    pieces = values.reshape(PEERS, LINES, 128)
    pieces = lax.all_to_all(
        pieces, ("gz", "gy"), 0, 0, tiled=True, axis_index_groups=RUN_PEERS
    )
    return pieces.reshape(512, 128)


def local(source, screening):
    even, odd, odd_t = (jnp.asarray(table) for table in half_tables())
    waves = wave_terms()
    gz, gy = lax.axis_index("gz"), lax.axis_index("gy")
    place = jnp.stack([gz // 8, (gz + 8 - FIRST_Y) % 8 * 8 + gy]).astype(jnp.int32)

    along_x = call(
        forward_x_kernel,
        [HBM] * 3,
        shape(512, 128),
        [
            pltpu.VMEM((2, 64, NX), F32),
            pltpu.VMEM((2 * HALF, HALF), BF16),
            pltpu.VMEM((2 * HALF, HALF), BF16),
            pltpu.SemaphoreType.DMA((3,)),
        ],
        name="forward_x",
        limit=60 * 1024 * 1024,
    )(source, even, odd)
    columns = exchange_peers(along_x)
    planes = shape(RUN, LINES, NY)
    pivots, up, down, far, close = call(
        pivots_kernel,
        [SMEM, SMEM, SMEM, VMEM],
        (planes, planes, planes, shape(CHUNKS, LINES, NY), shape(LINES, NY)),
        [pltpu.VMEM((2, LINES, NY), F32)],
        name="pivots",
    )(place, screening, jnp.asarray(waves), jnp.asarray(waves)[None, :])
    modes, send = call(
        forward_y_kernel,
        [SMEM] + [VMEM] * 5,
        (planes, shape(CHUNKS, LINES, NY)),
        name="forward_y",
    )(place, columns, even, odd_t, up, down)
    arrived = lax.all_to_all(send, "gz", 0, 0, tiled=True, axis_index_groups=RUNS)
    back_y = call(
        solve_kernel,
        [SMEM] + [VMEM] * 7,
        shape(8, 8, LINES, 128),
        [pltpu.VMEM((RUN, LINES, NY), F32)],
        name="solve",
    )(place, modes, arrived, pivots, far, close, even, odd)
    rows = exchange_peers(back_y)
    return call(backward_x_kernel, [VMEM] * 3, shape(2, 64, NX), name="backward_x")(
        rows, even, odd
    )


def solution(mesh):
    in_specs = (P("gz", "gy", None), P())
    out_specs = P("gz", "gy", None)
    return jax.shard_map(local, mesh=mesh, in_specs=in_specs, out_specs=out_specs, check_vma=False)
```

```python
import math

import jax
import jax.numpy as jnp
import ml_dtypes
import numpy as np
from jax import lax
from jax.experimental import pallas as pl
from jax.experimental.pallas import tpu as pltpu
from jax.sharding import PartitionSpec as P

NX = 512
NY = 512
NZ = 128
HALF = 256
CHUNKS = 8
RUN = NZ // CHUNKS
LINES = 8
PEERS = 64
FIRST_RUN = 4
FIRST_Y = 4

F32 = jnp.float32
BF16 = jnp.bfloat16


def split_table(table):
    high = table.astype(ml_dtypes.bfloat16)
    low = (table - high.astype(np.float64)).astype(ml_dtypes.bfloat16)
    return np.concatenate([high, low], axis=0)


def cas(rows, columns, total):
    angle = (rows[:, None] * columns[None, :] % total) * (2.0 * math.pi / total)
    return np.cos(angle) + np.sin(angle)


def half_tables():
    index = np.arange(HALF)
    even = cas(2 * index, index, 2 * HALF)
    odd = cas(2 * index + 1, index, 2 * HALF)
    return split_table(even), split_table(odd), split_table(odd.T)


def wave_terms():
    index = np.concatenate([np.arange(0, 512, 2), np.arange(1, 512, 2)])
    return (4.0 * np.sin(index * (math.pi / 512)) ** 2).astype(np.float32)


def split(values):
    high = values.astype(BF16)
    low = (values - high.astype(F32)).astype(BF16)
    return high, low


def times_table(values, table_ref):
    rows = values.shape[0]
    high, low = split(values)
    both = jnp.concatenate([high, low], axis=0)
    main = jnp.dot(both, table_ref[:HALF], preferred_element_type=F32)
    rest = jnp.dot(high, table_ref[HALF:], preferred_element_type=F32)
    return main[:rows] + (main[rows:] + rest)


def table_times_transposed(table_ref, values):
    rows = values.shape[0]
    high, low = split(values)
    both = jnp.concatenate([high, low], axis=0)
    product = lax.dot_general(
        table_ref[...], both, (((1,), (1,)), ((), ())), preferred_element_type=F32
    )
    return product[:HALF, :rows] + (product[:HALF, rows:] + product[HALF:, :rows])


def row(plane):
    return (plane - 2 * FIRST_Y) % RUN


def place_of_run(run):
    return (run - FIRST_RUN) % CHUNKS


def forward_x_kernel(source_hbm, even_hbm, odd_hbm, out_ref, source_ref, even_ref, odd_ref, arrived):
    copies = [
        pltpu.make_async_copy(source_hbm, source_ref, arrived.at[0]),
        pltpu.make_async_copy(even_hbm, even_ref, arrived.at[1]),
        pltpu.make_async_copy(odd_hbm, odd_ref, arrived.at[2]),
    ]
    for copy in copies:
        copy.start()
    copies[0].wait()
    rows = source_ref[...].reshape(128, NX)
    low, high = rows[:, :HALF], rows[:, HALF:]
    copies[1].wait()
    out_ref[:HALF] = table_times_transposed(even_ref, low + high)
    copies[2].wait()
    out_ref[HALF:] = table_times_transposed(odd_ref, low - high)


def pivots_kernel(place_ref, screening_ref, wave_k_ref, wave_l_ref, pivot_ref, up_ref, down_ref, far_ref, close_ref, chunk_ref, state_ref):
    chunk, group = place_ref[0], place_ref[1]
    chunk_ref[...] = jnp.zeros((LINES, NY), jnp.int32) + chunk
    line = lax.broadcasted_iota(jnp.int32, (LINES, NY), 0)
    lam = jnp.zeros((LINES, NY), F32) + wave_l_ref[...]
    for k in range(LINES):
        lam = lam + jnp.where(line == k, wave_k_ref[group * LINES + k], 0.0)
    one = jnp.ones((LINES, NY), F32)

    def step(plane, total, rise):
        rise = rise + (screening_ref[plane] + lam) * total
        return total + rise, rise

    def lap(index, state):
        below, above = state
        other = CHUNKS - 1 - index

        @pl.when(index == chunk)
        def _():
            state_ref[0] = below

        @pl.when(other == chunk)
        def _():
            state_ref[1] = above

        low_total, low_rise, high_total, high_rise = one, below, one, above
        for t in range(RUN):
            low_total, low_rise = step(index * RUN + t, low_total, low_rise)
            high_total, high_rise = step(other * RUN + RUN - 1 - t, high_total, high_rise)
        low_inverse, high_inverse = 1.0 / low_total, 1.0 / high_total

        @pl.when(index < chunk)
        def _():
            far_ref[index] = low_inverse

        @pl.when(other > chunk)
        def _():
            far_ref[other] = high_inverse

        return low_rise * low_inverse, high_rise * high_inverse

    far_ref[chunk] = jnp.zeros((LINES, NY), F32)
    lax.fori_loop(0, CHUNKS, lap, (one, one))

    first = chunk * RUN
    total, rise = one, state_ref[0]
    for t in range(RUN):
        up_ref[t] = total
        before = total
        total, rise = step(first + t, total, rise)
        pivot_ref[t] = before / total
    inverse = 1.0 / total
    last_pivot = pivot_ref[RUN - 1]
    close_ref[...] = 1.0 / (rise * inverse + last_pivot * state_ref[1])
    for t in range(RUN):
        up_ref[t] = up_ref[t] * inverse

    total, rise = one, state_ref[1]
    for t in reversed(range(RUN)):
        down_ref[t] = total
        total, rise = step(first + t, total, rise)
    inverse = 1.0 / total
    for t in range(RUN):
        down_ref[t] = down_ref[t] * inverse


def swap_halves(values):
    shape = values.shape
    return pltpu.roll(values.reshape(-1, 128), 64, 1).reshape(shape)


def lower_half(shape):
    return lax.broadcasted_iota(jnp.int32, shape, len(shape) - 1) < 64


def forward_y_kernel(chunk_ref, rows_ref, even_ref, odd_t_ref, up_ref, down_ref, modes_ref, send_ref):
    blocks = rows_ref[...].reshape(8, 8, LINES, 128)
    keep = lower_half((8, LINES, 128))

    def gather(parts):
        columns = []
        for pair in range(2):
            a, b = parts[2 * pair], parts[2 * pair + 1]
            first = jnp.where(keep, a, swap_halves(b))
            second = jnp.where(keep, swap_halves(a), b)
            columns.append(jnp.stack([first, second], axis=1).reshape(128, 128))
        return jnp.concatenate(columns, axis=1)

    sums = gather([blocks[:, g] + blocks[:, g + 4] for g in range(4)])
    differences = gather([blocks[:, g] - blocks[:, g + 4] for g in range(4)])
    modes_ref[:, :, :HALF] = times_table(sums, even_ref).reshape(RUN, LINES, HALF)
    modes_ref[:, :, HALF:] = times_table(differences, odd_t_ref).reshape(RUN, LINES, HALF)

    upward = jnp.zeros((LINES, NY), F32)
    downward = jnp.zeros((LINES, NY), F32)
    for t in range(RUN):
        plane = modes_ref[row(t)]
        upward = upward + up_ref[t] * plane
        downward = downward + down_ref[t] * plane
    chunk = chunk_ref[...]
    for other in range(CHUNKS):
        send_ref[place_of_run(other)] = jnp.where(other > chunk, upward, downward)


def solve_kernel(chunk_ref, modes_ref, arrived_ref, pivot_ref, far_ref, close_ref, even_ref, odd_ref, out_ref, solved_ref):
    chunk = chunk_ref[...]
    below = jnp.zeros((LINES, NY), F32)
    above = jnp.zeros((LINES, NY), F32)
    for other in range(CHUNKS):
        below = jnp.where(other < chunk, arrived_ref[place_of_run(other)] + far_ref[other] * below, below)
        rest = CHUNKS - 1 - other
        above = jnp.where(rest > chunk, arrived_ref[place_of_run(rest)] + far_ref[rest] * above, above)

    elimination = below
    for t in range(RUN):
        elimination = pivot_ref[t] * (modes_ref[row(t)] + elimination)
        solved_ref[row(t)] = elimination
    value = (elimination + pivot_ref[RUN - 1] * above) * close_ref[...]
    solved_ref[row(RUN - 1)] = value
    for t in reversed(range(RUN - 1)):
        value = solved_ref[row(t)] + pivot_ref[t] * value
        solved_ref[row(t)] = value

    solved = solved_ref[...].reshape(128, NY)
    even = times_table(solved[:, :HALF], even_ref)
    odd = times_table(solved[:, HALF:], odd_ref)
    keep = lower_half((8, LINES, 128))
    for base, values in ((0, even + odd), (4, even - odd)):
        for pair in range(2):
            column = values[:, pair * 128 : pair * 128 + 128].reshape(8, 2, LINES, 128)
            a, b = column[:, 0], column[:, 1]
            out_ref[:, base + 2 * pair] = jnp.where(keep, a, swap_halves(b))
            out_ref[:, base + 2 * pair + 1] = jnp.where(keep, swap_halves(a), b)


def backward_x_kernel(rows_ref, even_ref, odd_ref, out_ref):
    values = rows_ref[...].T
    even = times_table(values[:, :HALF], even_ref)
    odd = times_table(values[:, HALF:], odd_ref)
    scale = 1.0 / (NX * NY)
    out_ref[:, :, :HALF] = ((even + odd) * scale).reshape(2, 64, HALF)
    out_ref[:, :, HALF:] = ((even - odd) * scale).reshape(2, 64, HALF)


VMEM = pl.BlockSpec(memory_space=pltpu.VMEM)
HBM = pl.BlockSpec(memory_space=pltpu.HBM)
SMEM = pl.BlockSpec(memory_space=pltpu.SMEM)


def call(kernel, ins, outs, scratch=(), name=None, limit=16 * 1024 * 1024):
    return pl.pallas_call(
        kernel,
        in_specs=ins,
        out_specs=jax.tree.map(lambda _: VMEM, outs),
        out_shape=outs,
        scratch_shapes=list(scratch),
        compiler_params=pltpu.CompilerParams(vmem_limit_bytes=limit),
        name=name,
    )


def shape(*sizes):
    return jax.ShapeDtypeStruct(sizes, F32)


RUN_PEERS = [
    [run * PEERS + (peer + FIRST_Y * 8) % PEERS for peer in range(PEERS)] for run in range(CHUNKS)
]
RUNS = [[(run + FIRST_RUN) % CHUNKS * 8 + y for run in range(CHUNKS)] for y in range(8)]


def exchange_peers(values):
    pieces = values.reshape(PEERS, LINES, 128)
    pieces = lax.all_to_all(
        pieces, ("gz", "gy"), 0, 0, tiled=True, axis_index_groups=RUN_PEERS
    )
    return pieces.reshape(512, 128)


def local(source, screening):
    even, odd, odd_t = (jnp.asarray(table) for table in half_tables())
    waves = wave_terms()
    gz, gy = lax.axis_index("gz"), lax.axis_index("gy")
    place = jnp.stack([gz // 8, (gz + 8 - FIRST_Y) % 8 * 8 + gy]).astype(jnp.int32)

    along_x = call(
        forward_x_kernel,
        [HBM] * 3,
        shape(512, 128),
        [
            pltpu.VMEM((2, 64, NX), F32),
            pltpu.VMEM((2 * HALF, HALF), BF16),
            pltpu.VMEM((2 * HALF, HALF), BF16),
            pltpu.SemaphoreType.DMA((3,)),
        ],
        name="forward_x",
        limit=60 * 1024 * 1024,
    )(source, even, odd)
    columns = exchange_peers(along_x)
    planes = shape(RUN, LINES, NY)
    whole = jax.ShapeDtypeStruct((LINES, NY), jnp.int32)
    pivots, up, down, far, close, chunk = call(
        pivots_kernel,
        [SMEM, SMEM, SMEM, VMEM],
        (planes, planes, planes, shape(CHUNKS, LINES, NY), shape(LINES, NY), whole),
        [pltpu.VMEM((2, LINES, NY), F32)],
        name="pivots",
    )(place, screening, jnp.asarray(waves), jnp.asarray(waves)[None, :])
    modes, send = call(
        forward_y_kernel,
        [VMEM] * 6,
        (planes, shape(CHUNKS, LINES, NY)),
        name="forward_y",
    )(chunk, columns, even, odd_t, up, down)
    arrived = lax.all_to_all(send, "gz", 0, 0, tiled=True, axis_index_groups=RUNS)
    back_y = call(
        solve_kernel,
        [VMEM] * 8,
        shape(8, 8, LINES, 128),
        [pltpu.VMEM((RUN, LINES, NY), F32)],
        name="solve",
    )(chunk, modes, arrived, pivots, far, close, even, odd)
    rows = exchange_peers(back_y)
    return call(backward_x_kernel, [VMEM] * 3, shape(2, 64, NX), name="backward_x")(
        rows, even, odd
    )


def solution(mesh):
    in_specs = (P("gz", "gy", None), P())
    out_specs = P("gz", "gy", None)
    return jax.shard_map(local, mesh=mesh, in_specs=in_specs, out_specs=out_specs, check_vma=False)
```

```python
import math

import jax
import jax.numpy as jnp
import ml_dtypes
import numpy as np
from jax import lax
from jax.experimental import pallas as pl
from jax.experimental.pallas import tpu as pltpu
from jax.sharding import PartitionSpec as P

NX = 512
NY = 512
NZ = 128
HALF = 256
CHUNKS = 8
RUN = NZ // CHUNKS
LINES = 8
PEERS = 64
RUN_ORDER = (4, 3, 5, 2, 6, 1, 7, 0)
Y_IN = (4, 5, 6, 7, 0, 1, 2, 3)
G_IN = (7, 0, 1, 2, 3, 4, 5, 6)
Y_OUT = (4, 5, 6, 7, 0, 1, 2, 3)
G_OUT = (5, 4, 7, 6, 1, 0, 3, 2)

F32 = jnp.float32
BF16 = jnp.bfloat16


def split_table(table):
    high = table.astype(ml_dtypes.bfloat16)
    low = (table - high.astype(np.float64)).astype(ml_dtypes.bfloat16)
    return np.concatenate([high, low], axis=0)


def cas(rows, columns, total):
    angle = (rows[:, None] * columns[None, :] % total) * (2.0 * math.pi / total)
    return np.cos(angle) + np.sin(angle)


def half_tables():
    index = np.arange(HALF)
    even = cas(2 * index, index, 2 * HALF)
    odd = cas(2 * index + 1, index, 2 * HALF)
    return split_table(even), split_table(odd), split_table(odd.T)


def wave_terms():
    index = np.concatenate([np.arange(0, 512, 2), np.arange(1, 512, 2)])
    return (4.0 * np.sin(index * (math.pi / 512)) ** 2).astype(np.float32)


def split(values):
    high = values.astype(BF16)
    low = (values - high.astype(F32)).astype(BF16)
    return high, low


def times_table(values, table_ref):
    rows = values.shape[0]
    high, low = split(values)
    both = jnp.concatenate([high, low], axis=0)
    main = jnp.dot(both, table_ref[:HALF], preferred_element_type=F32)
    rest = jnp.dot(high, table_ref[HALF:], preferred_element_type=F32)
    return main[:rows] + (main[rows:] + rest)


def table_times_transposed(table_ref, values):
    rows = values.shape[0]
    high, low = split(values)
    both = jnp.concatenate([high, low], axis=0)
    product = lax.dot_general(
        table_ref[...], both, (((1,), (1,)), ((), ())), preferred_element_type=F32
    )
    return product[:HALF, :rows] + (product[:HALF, rows:] + product[HALF:, :rows])


def row(plane, order):
    return 2 * order.index(plane // 2) + plane % 2


def forward_x_kernel(source_hbm, even_hbm, odd_hbm, out_ref, source_ref, even_ref, odd_ref, arrived):
    copies = [
        pltpu.make_async_copy(source_hbm, source_ref, arrived.at[0]),
        pltpu.make_async_copy(even_hbm, even_ref, arrived.at[1]),
        pltpu.make_async_copy(odd_hbm, odd_ref, arrived.at[2]),
    ]
    for copy in copies:
        copy.start()
    for copy in copies:
        copy.wait()
    rows = source_ref[...].reshape(128, NX)
    low, high = rows[:, :HALF], rows[:, HALF:]
    out_ref[:HALF] = table_times_transposed(even_ref, low + high)
    out_ref[HALF:] = table_times_transposed(odd_ref, low - high)


def pivots_kernel(place_ref, screening_ref, wave_k_ref, wave_l_ref, pivot_ref, up_ref, down_ref, far_ref, close_ref, chunk_ref, state_ref):
    chunk, group = place_ref[0], place_ref[1]
    chunk_ref[...] = jnp.zeros((LINES, NY), jnp.int32) + chunk
    line = lax.broadcasted_iota(jnp.int32, (LINES, NY), 0)
    lam = jnp.zeros((LINES, NY), F32) + wave_l_ref[...]
    for k in range(LINES):
        lam = lam + jnp.where(line == k, wave_k_ref[group * LINES + k], 0.0)
    one = jnp.ones((LINES, NY), F32)

    def step(plane, total, rise):
        rise = rise + (screening_ref[plane] + lam) * total
        return total + rise, rise

    def lap(index, state):
        below, above = state
        other = CHUNKS - 1 - index

        @pl.when(index == chunk)
        def _():
            state_ref[0] = below

        @pl.when(other == chunk)
        def _():
            state_ref[1] = above

        low_total, low_rise, high_total, high_rise = one, below, one, above
        for t in range(RUN):
            low_total, low_rise = step(index * RUN + t, low_total, low_rise)
            high_total, high_rise = step(other * RUN + RUN - 1 - t, high_total, high_rise)
        low_inverse, high_inverse = 1.0 / low_total, 1.0 / high_total

        @pl.when(index < chunk)
        def _():
            far_ref[index] = low_inverse

        @pl.when(other > chunk)
        def _():
            far_ref[other] = high_inverse

        return low_rise * low_inverse, high_rise * high_inverse

    far_ref[chunk] = jnp.zeros((LINES, NY), F32)
    lax.fori_loop(0, CHUNKS, lap, (one, one))

    first = chunk * RUN
    total, rise = one, state_ref[0]
    for t in range(RUN):
        up_ref[t] = total
        before = total
        total, rise = step(first + t, total, rise)
        pivot_ref[t] = before / total
    inverse = 1.0 / total
    last_pivot = pivot_ref[RUN - 1]
    close_ref[...] = 1.0 / (rise * inverse + last_pivot * state_ref[1])
    for t in range(RUN):
        up_ref[t] = up_ref[t] * inverse

    total, rise = one, state_ref[1]
    for t in reversed(range(RUN)):
        down_ref[t] = total
        total, rise = step(first + t, total, rise)
    inverse = 1.0 / total
    for t in range(RUN):
        down_ref[t] = down_ref[t] * inverse


def swap_halves(values):
    shape = values.shape
    return pltpu.roll(values.reshape(-1, 128), 64, 1).reshape(shape)


def lower_half(shape):
    return lax.broadcasted_iota(jnp.int32, shape, len(shape) - 1) < 64


def forward_y_kernel(chunk_ref, rows_ref, even_ref, odd_t_ref, up_ref, down_ref, modes_ref, send_ref):
    blocks = rows_ref[...].reshape(8, 8, LINES, 128)
    keep = lower_half((8, LINES, 128))

    def at(g):
        return blocks[:, G_IN.index(g)]

    def gather(parts):
        columns = []
        for pair in range(2):
            a, b = parts[2 * pair], parts[2 * pair + 1]
            first = jnp.where(keep, a, swap_halves(b))
            second = jnp.where(keep, swap_halves(a), b)
            columns.append(jnp.stack([first, second], axis=1).reshape(128, 128))
        return jnp.concatenate(columns, axis=1)

    sums = gather([at(g) + at(g + 4) for g in range(4)])
    differences = gather([at(g) - at(g + 4) for g in range(4)])
    modes_ref[:, :, :HALF] = times_table(sums, even_ref).reshape(RUN, LINES, HALF)
    modes_ref[:, :, HALF:] = times_table(differences, odd_t_ref).reshape(RUN, LINES, HALF)

    upward = jnp.zeros((LINES, NY), F32)
    downward = jnp.zeros((LINES, NY), F32)
    for t in range(RUN):
        plane = modes_ref[row(t, Y_IN)]
        upward = upward + up_ref[t] * plane
        downward = downward + down_ref[t] * plane
    chunk = chunk_ref[...]
    for other in range(CHUNKS):
        send_ref[RUN_ORDER.index(other)] = jnp.where(other > chunk, upward, downward)


def solve_kernel(chunk_ref, modes_ref, arrived_ref, pivot_ref, far_ref, close_ref, even_ref, odd_ref, out_ref, solved_ref):
    chunk = chunk_ref[...]
    below = jnp.zeros((LINES, NY), F32)
    above = jnp.zeros((LINES, NY), F32)
    for other in range(CHUNKS):
        below = jnp.where(other < chunk, arrived_ref[RUN_ORDER.index(other)] + far_ref[other] * below, below)
        rest = CHUNKS - 1 - other
        above = jnp.where(rest > chunk, arrived_ref[RUN_ORDER.index(rest)] + far_ref[rest] * above, above)

    elimination = below
    for t in range(RUN):
        elimination = pivot_ref[t] * (modes_ref[row(t, Y_IN)] + elimination)
        solved_ref[row(t, Y_OUT)] = elimination
    value = (elimination + pivot_ref[RUN - 1] * above) * close_ref[...]
    solved_ref[row(RUN - 1, Y_OUT)] = value
    for t in reversed(range(RUN - 1)):
        value = solved_ref[row(t, Y_OUT)] + pivot_ref[t] * value
        solved_ref[row(t, Y_OUT)] = value

    solved = solved_ref[...].reshape(128, NY)
    even = times_table(solved[:, :HALF], even_ref)
    odd = times_table(solved[:, HALF:], odd_ref)
    keep = lower_half((8, LINES, 128))
    for base, values in ((0, even + odd), (4, even - odd)):
        for pair in range(2):
            column = values[:, pair * 128 : pair * 128 + 128].reshape(8, 2, LINES, 128)
            a, b = column[:, 0], column[:, 1]
            out_ref[:, G_OUT.index(base + 2 * pair)] = jnp.where(keep, a, swap_halves(b))
            out_ref[:, G_OUT.index(base + 2 * pair + 1)] = jnp.where(keep, swap_halves(a), b)


def backward_x_kernel(rows_ref, even_ref, odd_ref, out_ref):
    blocks = rows_ref[...].reshape(8, 8, LINES, 128)
    ordered = [blocks[Y_OUT.index(y), G_OUT.index(g)] for y in Y_IN for g in G_IN]
    values = jnp.concatenate(ordered, axis=0).T
    even = times_table(values[:, :HALF], even_ref)
    odd = times_table(values[:, HALF:], odd_ref)
    scale = 1.0 / (NX * NY)
    out_ref[:, :, :HALF] = ((even + odd) * scale).reshape(2, 64, HALF)
    out_ref[:, :, HALF:] = ((even - odd) * scale).reshape(2, 64, HALF)


VMEM = pl.BlockSpec(memory_space=pltpu.VMEM)
HBM = pl.BlockSpec(memory_space=pltpu.HBM)
SMEM = pl.BlockSpec(memory_space=pltpu.SMEM)


def call(kernel, ins, outs, scratch=(), name=None, limit=16 * 1024 * 1024):
    return pl.pallas_call(
        kernel,
        in_specs=ins,
        out_specs=jax.tree.map(lambda _: VMEM, outs),
        out_shape=outs,
        scratch_shapes=list(scratch),
        compiler_params=pltpu.CompilerParams(vmem_limit_bytes=limit),
        name=name,
    )


def shape(*sizes):
    return jax.ShapeDtypeStruct(sizes, F32)


def run_peers(along_y, along_g):
    return [[run * PEERS + y * 8 + g for y in along_y for g in along_g] for run in range(CHUNKS)]


RUNS = [[run * 8 + y for run in RUN_ORDER] for y in range(8)]


def exchange_peers(values, along_y, along_g):
    pieces = values.reshape(PEERS, LINES, 128)
    pieces = lax.all_to_all(
        pieces, ("gz", "gy"), 0, 0, tiled=True, axis_index_groups=run_peers(along_y, along_g)
    )
    return pieces.reshape(512, 128)


def local(source, screening):
    even, odd, odd_t = (jnp.asarray(table) for table in half_tables())
    waves = wave_terms()
    gz, gy = lax.axis_index("gz"), lax.axis_index("gy")
    place_y = jnp.asarray([Y_IN.index(y) for y in range(8)], jnp.int32)[gz % 8]
    place_g = jnp.asarray([G_IN.index(g) for g in range(8)], jnp.int32)[gy]
    place = jnp.stack([gz // 8, place_y * 8 + place_g]).astype(jnp.int32)

    along_x = call(
        forward_x_kernel,
        [HBM] * 3,
        shape(512, 128),
        [
            pltpu.VMEM((2, 64, NX), F32),
            pltpu.VMEM((2 * HALF, HALF), BF16),
            pltpu.VMEM((2 * HALF, HALF), BF16),
            pltpu.SemaphoreType.DMA((3,)),
        ],
        name="forward_x",
        limit=60 * 1024 * 1024,
    )(source, even, odd)
    columns = exchange_peers(along_x, Y_IN, G_IN)
    planes = shape(RUN, LINES, NY)
    whole = jax.ShapeDtypeStruct((LINES, NY), jnp.int32)
    pivots, up, down, far, close, chunk = call(
        pivots_kernel,
        [SMEM, SMEM, SMEM, VMEM],
        (planes, planes, planes, shape(CHUNKS, LINES, NY), shape(LINES, NY), whole),
        [pltpu.VMEM((2, LINES, NY), F32)],
        name="pivots",
    )(place, screening, jnp.asarray(waves), jnp.asarray(waves)[None, :])
    modes, send = call(
        forward_y_kernel,
        [VMEM] * 6,
        (planes, shape(CHUNKS, LINES, NY)),
        name="forward_y",
    )(chunk, columns, even, odd_t, up, down)
    arrived = lax.all_to_all(send, "gz", 0, 0, tiled=True, axis_index_groups=RUNS)
    back_y = call(
        solve_kernel,
        [VMEM] * 8,
        shape(8, 8, LINES, 128),
        [pltpu.VMEM((RUN, LINES, NY), F32)],
        name="solve",
    )(chunk, modes, arrived, pivots, far, close, even, odd)
    rows = exchange_peers(back_y, Y_OUT, G_OUT)
    return call(backward_x_kernel, [VMEM] * 3, shape(2, 64, NX), name="backward_x")(
        rows, even, odd
    )


def solution(mesh):
    in_specs = (P("gz", "gy", None), P())
    out_specs = P("gz", "gy", None)
    return jax.shard_map(local, mesh=mesh, in_specs=in_specs, out_specs=out_specs, check_vma=False)
```

```python
import math

import jax
import jax.numpy as jnp
import ml_dtypes
import numpy as np
from jax import lax
from jax.experimental import pallas as pl
from jax.experimental.pallas import tpu as pltpu
from jax.sharding import PartitionSpec as P

NX = 512
NY = 512
NZ = 128
HALF = 256
CHUNKS = 8
RUN = NZ // CHUNKS
LINES = 8
PEERS = 64
RUN_ORDER = (4, 3, 5, 2, 6, 1, 7, 0)
Y_IN = (4, 5, 6, 7, 0, 1, 2, 3)
G_IN = (7, 0, 1, 2, 3, 4, 5, 6)
Y_OUT = (4, 5, 6, 7, 0, 1, 2, 3)
G_OUT = (5, 4, 7, 6, 1, 0, 3, 2)

X_KERNEL_VMEM = 55574528

F32 = jnp.float32
BF16 = jnp.bfloat16


def split_table(table):
    high = table.astype(ml_dtypes.bfloat16)
    low = (table - high.astype(np.float64)).astype(ml_dtypes.bfloat16)
    return np.concatenate([high, low], axis=0)


def cas(rows, columns, total):
    angle = (rows[:, None] * columns[None, :] % total) * (2.0 * math.pi / total)
    return np.cos(angle) + np.sin(angle)


def half_tables():
    index = np.arange(HALF)
    even = cas(2 * index, index, 2 * HALF)
    odd = cas(2 * index + 1, index, 2 * HALF)
    return split_table(even), split_table(odd), split_table(odd.T)


def wave_terms():
    index = np.concatenate([np.arange(0, 512, 2), np.arange(1, 512, 2)])
    return (4.0 * np.sin(index * (math.pi / 512)) ** 2).astype(np.float32).reshape(4, 128)


def split(values):
    high = values.astype(BF16)
    low = (values - high.astype(F32)).astype(BF16)
    return high, low


def times_table(values, table_ref):
    rows = values.shape[0]
    high, low = split(values)
    both = jnp.concatenate([high, low], axis=0)
    main = jnp.dot(both, table_ref[:HALF], preferred_element_type=F32)
    rest = jnp.dot(high, table_ref[HALF:], preferred_element_type=F32)
    return main[:rows] + (main[rows:] + rest)


def table_times_transposed(table_ref, values):
    rows = values.shape[0]
    high, low = split(values)
    both = jnp.concatenate([high, low], axis=0)
    product = lax.dot_general(
        table_ref[...], both, (((1,), (1,)), ((), ())), preferred_element_type=F32
    )
    return product[:HALF, :rows] + (product[:HALF, rows:] + product[HALF:, :rows])


def row(plane, order):
    return 2 * order.index(plane // 2) + plane % 2


def own_place():
    gz, gy = lax.axis_index("gz"), lax.axis_index("gy")
    return gz >> 3, (((gz & 7) + 8 - Y_IN[0]) & 7) * 8 + ((gy + 8 - G_IN[0]) & 7)


def pivots(screening_ref, waves_ref, shift_ref, column_ref, pivot_ref, down_ref, far_ref, close_ref, chunk_ref):
    chunk, group = own_place()
    chunk_ref[...] = jnp.zeros((LINES, NY), jnp.int32) + chunk
    shift_ref[...] = jnp.broadcast_to(screening_ref[...], (NZ, NZ)).T
    column_ref[...] = jnp.broadcast_to(waves_ref[pl.ds(group >> 4, 1), :], (128, 128)).T
    along_k = column_ref[pl.ds(pl.multiple_of((group & 15) * LINES, LINES), LINES), :]
    lam = jnp.concatenate([waves_ref[q : q + 1, :] + along_k for q in range(4)], axis=1)
    one = jnp.ones((LINES, NY), F32)

    def step(plane, total, rise):
        shift = shift_ref[pl.ds(plane, 1), :]
        rise = rise + (jnp.concatenate([shift] * 4, axis=1) + lam) * total
        return total + rise, rise

    below, above = one, one
    own_below, own_above = one, one
    for index in range(CHUNKS - 1):
        other = CHUNKS - 1 - index
        low_total, low_rise, high_total, high_rise = one, below, one, above
        for t in range(RUN):
            low_total, low_rise = step(index * RUN + t, low_total, low_rise)
            high_total, high_rise = step(other * RUN + RUN - 1 - t, high_total, high_rise)
        low_inverse, high_inverse = 1.0 / low_total, 1.0 / high_total

        @pl.when(index < chunk)
        def _():
            far_ref[index] = low_inverse

        @pl.when(other > chunk)
        def _():
            far_ref[other] = high_inverse

        below, above = low_rise * low_inverse, high_rise * high_inverse
        own_below = jnp.where(chunk == index + 1, below, own_below)
        own_above = jnp.where(chunk == other - 1, above, own_above)
    far_ref[chunk] = jnp.zeros((LINES, NY), F32)

    first = chunk * RUN
    total, rise, high_total, high_rise = one, own_below, one, own_above
    for t in range(RUN):
        down_ref[RUN - 1 - t] = high_total
        before = total
        total, rise = step(first + t, total, rise)
        pivot_ref[t] = before / total
        high_total, high_rise = step(first + RUN - 1 - t, high_total, high_rise)
    inverse = 1.0 / total
    close_ref[...] = 1.0 / (rise * inverse + pivot_ref[RUN - 1] * own_above)
    high_inverse = 1.0 / high_total
    for t in range(RUN):
        down_ref[t] = down_ref[t] * high_inverse


def forward_x_kernel(
    screening_ref, waves_ref, source_hbm, even_hbm, odd_hbm,
    out_ref, pivot_ref, down_ref, far_ref, close_ref, chunk_ref,
    source_ref, even_ref, odd_ref, shift_ref, column_ref, arrived,
):
    copies = [
        pltpu.make_async_copy(source_hbm, source_ref, arrived.at[0]),
        pltpu.make_async_copy(even_hbm, even_ref, arrived.at[1]),
        pltpu.make_async_copy(odd_hbm, odd_ref, arrived.at[2]),
    ]
    for copy in copies:
        copy.start()
    pivots(
        screening_ref, waves_ref, shift_ref, column_ref,
        pivot_ref, down_ref, far_ref, close_ref, chunk_ref,
    )
    for copy in copies:
        copy.wait()
    rows = source_ref[...].reshape(128, NX)
    low, high = rows[:, :HALF], rows[:, HALF:]
    out_ref[:HALF] = table_times_transposed(even_ref, low + high)
    out_ref[HALF:] = table_times_transposed(odd_ref, low - high)


def swap_halves(values):
    shape = values.shape
    return pltpu.roll(values.reshape(-1, 128), 64, 1).reshape(shape)


def lower_half(shape):
    return lax.broadcasted_iota(jnp.int32, shape, len(shape) - 1) < 64


def forward_y_kernel(chunk_ref, rows_ref, even_ref, odd_t_ref, pivot_ref, down_ref, modes_ref, send_ref):
    blocks = rows_ref[...].reshape(8, 8, LINES, 128)
    keep = lower_half((8, LINES, 128))

    def at(g):
        return blocks[:, G_IN.index(g)]

    def gather(parts):
        columns = []
        for pair in range(2):
            a, b = parts[2 * pair], parts[2 * pair + 1]
            first = jnp.where(keep, a, swap_halves(b))
            second = jnp.where(keep, swap_halves(a), b)
            columns.append(jnp.stack([first, second], axis=1).reshape(128, 128))
        return jnp.concatenate(columns, axis=1)

    sums = gather([at(g) + at(g + 4) for g in range(4)])
    differences = gather([at(g) - at(g + 4) for g in range(4)])
    modes_ref[:, :, :HALF] = times_table(sums, even_ref).reshape(RUN, LINES, HALF)
    modes_ref[:, :, HALF:] = times_table(differences, odd_t_ref).reshape(RUN, LINES, HALF)

    upward = jnp.zeros((LINES, NY), F32)
    downward = jnp.zeros((LINES, NY), F32)
    for t in range(RUN):
        plane = modes_ref[row(t, Y_IN)]
        upward = pivot_ref[t] * (plane + upward)
        downward = downward + down_ref[t] * plane
    chunk = chunk_ref[...]
    for other in range(CHUNKS):
        send_ref[RUN_ORDER.index(other)] = jnp.where(other > chunk, upward, downward)


def solve_kernel(chunk_ref, modes_ref, arrived_ref, pivot_ref, far_ref, close_ref, even_ref, odd_ref, out_ref, solved_ref):
    chunk = chunk_ref[...]
    below = jnp.zeros((LINES, NY), F32)
    above = jnp.zeros((LINES, NY), F32)
    for other in range(CHUNKS):
        below = jnp.where(other < chunk, arrived_ref[RUN_ORDER.index(other)] + far_ref[other] * below, below)
        rest = CHUNKS - 1 - other
        above = jnp.where(rest > chunk, arrived_ref[RUN_ORDER.index(rest)] + far_ref[rest] * above, above)

    elimination = below
    for t in range(RUN):
        elimination = pivot_ref[t] * (modes_ref[row(t, Y_IN)] + elimination)
        solved_ref[row(t, Y_OUT)] = elimination
    value = (elimination + pivot_ref[RUN - 1] * above) * close_ref[...]
    solved_ref[row(RUN - 1, Y_OUT)] = value
    for t in reversed(range(RUN - 1)):
        value = solved_ref[row(t, Y_OUT)] + pivot_ref[t] * value
        solved_ref[row(t, Y_OUT)] = value

    solved = solved_ref[...].reshape(128, NY)
    even = times_table(solved[:, :HALF], even_ref)
    odd = times_table(solved[:, HALF:], odd_ref)
    keep = lower_half((8, LINES, 128))
    for base, values in ((0, even + odd), (4, even - odd)):
        for pair in range(2):
            column = values[:, pair * 128 : pair * 128 + 128].reshape(8, 2, LINES, 128)
            a, b = column[:, 0], column[:, 1]
            out_ref[:, G_OUT.index(base + 2 * pair)] = jnp.where(keep, a, swap_halves(b))
            out_ref[:, G_OUT.index(base + 2 * pair + 1)] = jnp.where(keep, swap_halves(a), b)


def backward_x_kernel(rows_ref, even_ref, odd_ref, out_ref):
    blocks = rows_ref[...].reshape(8, 8, LINES, 128)
    ordered = [blocks[Y_OUT.index(y), G_OUT.index(g)] for y in Y_IN for g in G_IN]
    values = jnp.concatenate(ordered, axis=0).T
    even = times_table(values[:, :HALF], even_ref)
    odd = times_table(values[:, HALF:], odd_ref)
    scale = 1.0 / (NX * NY)
    out_ref[:, :, :HALF] = ((even + odd) * scale).reshape(2, 64, HALF)
    out_ref[:, :, HALF:] = ((even - odd) * scale).reshape(2, 64, HALF)


VMEM = pl.BlockSpec(memory_space=pltpu.VMEM)
HBM = pl.BlockSpec(memory_space=pltpu.HBM)
SMEM = pl.BlockSpec(memory_space=pltpu.SMEM)


def call(kernel, ins, outs, scratch=(), name=None, limit=16 * 1024 * 1024):
    return pl.pallas_call(
        kernel,
        in_specs=ins,
        out_specs=jax.tree.map(lambda _: VMEM, outs),
        out_shape=outs,
        scratch_shapes=list(scratch),
        compiler_params=pltpu.CompilerParams(vmem_limit_bytes=limit),
        name=name,
    )


def shape(*sizes):
    return jax.ShapeDtypeStruct(sizes, F32)


def run_peers(along_y, along_g):
    return [[run * PEERS + y * 8 + g for y in along_y for g in along_g] for run in range(CHUNKS)]


RUNS = [[run * 8 + y for run in RUN_ORDER] for y in range(8)]


def exchange_peers(values, along_y, along_g):
    pieces = values.reshape(PEERS, LINES, 128)
    pieces = lax.all_to_all(
        pieces, ("gz", "gy"), 0, 0, tiled=True, axis_index_groups=run_peers(along_y, along_g)
    )
    return pieces.reshape(512, 128)


def local(source, screening):
    even, odd, odd_t = (jnp.asarray(table) for table in half_tables())
    waves = wave_terms()
    planes = shape(RUN, LINES, NY)
    whole = jax.ShapeDtypeStruct((LINES, NY), jnp.int32)
    along_x, pivot, down, far, close, chunk = call(
        forward_x_kernel,
        [VMEM] * 2 + [HBM] * 3,
        (shape(512, 128), planes, planes, shape(CHUNKS, LINES, NY), shape(LINES, NY), whole),
        [
            pltpu.VMEM((2, 64, NX), F32),
            pltpu.VMEM((2 * HALF, HALF), BF16),
            pltpu.VMEM((2 * HALF, HALF), BF16),
            pltpu.VMEM((NZ, NZ), F32),
            pltpu.VMEM((128, 128), F32),
            pltpu.SemaphoreType.DMA((3,)),
        ],
        name="forward_x",
        limit=X_KERNEL_VMEM,
    )(screening[None, :], jnp.asarray(waves), source, even, odd)
    columns = exchange_peers(along_x, Y_IN, G_IN)
    modes, send = call(
        forward_y_kernel,
        [VMEM] * 6,
        (planes, shape(CHUNKS, LINES, NY)),
        name="forward_y",
    )(chunk, columns, even, odd_t, pivot, down)
    arrived = lax.all_to_all(send, "gz", 0, 0, tiled=True, axis_index_groups=RUNS)
    back_y = call(
        solve_kernel,
        [VMEM] * 8,
        shape(8, 8, LINES, 128),
        [pltpu.VMEM((RUN, LINES, NY), F32)],
        name="solve",
    )(chunk, modes, arrived, pivot, far, close, even, odd)
    rows = exchange_peers(back_y, Y_OUT, G_OUT)
    return call(backward_x_kernel, [VMEM] * 3, shape(2, 64, NX), name="backward_x")(
        rows, even, odd
    )


def solution(mesh):
    in_specs = (P("gz", "gy", None), P())
    out_specs = P("gz", "gy", None)
    return jax.shard_map(local, mesh=mesh, in_specs=in_specs, out_specs=out_specs, check_vma=False)
```

```python
import math

import jax
import jax.numpy as jnp
import ml_dtypes
import numpy as np
from jax import lax
from jax.experimental import pallas as pl
from jax.experimental.pallas import tpu as pltpu
from jax.sharding import PartitionSpec as P

NX = 512
NY = 512
NZ = 128
HALF = 256
CHUNKS = 8
RUN = NZ // CHUNKS
LINES = 8
PEERS = 64
RUN_ORDER = (4, 3, 5, 2, 6, 1, 7, 0)
Y_IN = (4, 5, 6, 7, 0, 1, 2, 3)
G_IN = (7, 0, 1, 2, 3, 4, 5, 6)
Y_OUT = (4, 5, 6, 7, 0, 1, 2, 3)
G_OUT = (5, 4, 7, 6, 1, 0, 3, 2)

X_KERNEL_VMEM = 55574528

F32 = jnp.float32
BF16 = jnp.bfloat16


def split_table(table):
    high = table.astype(ml_dtypes.bfloat16)
    low = (table - high.astype(np.float64)).astype(ml_dtypes.bfloat16)
    return np.concatenate([high, low], axis=0)


def cas(rows, columns, total):
    angle = (rows[:, None] * columns[None, :] % total) * (2.0 * math.pi / total)
    return np.cos(angle) + np.sin(angle)


def half_tables():
    index = np.arange(HALF)
    even = cas(2 * index, index, 2 * HALF)
    odd = cas(2 * index + 1, index, 2 * HALF)
    return split_table(even), split_table(odd), split_table(odd.T)


def wave_terms():
    index = np.concatenate([np.arange(0, 512, 2), np.arange(1, 512, 2)])
    return (4.0 * np.sin(index * (math.pi / 512)) ** 2).astype(np.float32).reshape(4, 128)


def split(values):
    high = values.astype(BF16)
    low = (values - high.astype(F32)).astype(BF16)
    return high, low


def times_table(values, table_ref):
    rows = values.shape[0]
    high, low = split(values)
    both = jnp.concatenate([high, low], axis=0)
    main = jnp.dot(both, table_ref[:HALF], preferred_element_type=F32)
    rest = jnp.dot(high, table_ref[HALF:], preferred_element_type=F32)
    return main[:rows] + (main[rows:] + rest)


def table_times_transposed(table_ref, values):
    rows = values.shape[0]
    high, low = split(values)
    both = jnp.concatenate([high, low], axis=0)
    product = lax.dot_general(
        table_ref[...], both, (((1,), (1,)), ((), ())), preferred_element_type=F32
    )
    return product[:HALF, :rows] + (product[:HALF, rows:] + product[HALF:, :rows])


def row(plane, order):
    return 2 * order.index(plane // 2) + plane % 2


def own_place():
    gz, gy = lax.axis_index("gz"), lax.axis_index("gy")
    return gz >> 3, ((gy + 8 - G_IN[0]) & 7) * 8 + (((gz & 7) + 8 - Y_IN[0]) & 7)


def pivots(screening_ref, waves_ref, shift_ref, column_ref, pivot_ref, down_ref, far_ref, close_ref, chunk_ref):
    chunk, group = own_place()
    chunk_ref[...] = jnp.zeros((LINES, NY), jnp.int32) + chunk
    shift_ref[...] = jnp.broadcast_to(screening_ref[...], (NZ, NZ)).T
    column_ref[...] = jnp.broadcast_to(waves_ref[pl.ds(group >> 4, 1), :], (128, 128)).T
    along_k = column_ref[pl.ds(pl.multiple_of((group & 15) * LINES, LINES), LINES), :]
    lam = jnp.concatenate([waves_ref[q : q + 1, :] + along_k for q in range(4)], axis=1)
    one = jnp.ones((LINES, NY), F32)

    def step(plane, total, rise):
        shift = shift_ref[pl.ds(plane, 1), :]
        rise = rise + (jnp.concatenate([shift] * 4, axis=1) + lam) * total
        return total + rise, rise

    below, above = one, one
    own_below, own_above = one, one
    for index in range(CHUNKS - 1):
        other = CHUNKS - 1 - index
        low_total, low_rise, high_total, high_rise = one, below, one, above
        for t in range(RUN):
            low_total, low_rise = step(index * RUN + t, low_total, low_rise)
            high_total, high_rise = step(other * RUN + RUN - 1 - t, high_total, high_rise)
        low_inverse, high_inverse = 1.0 / low_total, 1.0 / high_total

        @pl.when(index < chunk)
        def _():
            far_ref[index] = low_inverse

        @pl.when(other > chunk)
        def _():
            far_ref[other] = high_inverse

        below, above = low_rise * low_inverse, high_rise * high_inverse
        own_below = jnp.where(chunk == index + 1, below, own_below)
        own_above = jnp.where(chunk == other - 1, above, own_above)
    far_ref[chunk] = jnp.zeros((LINES, NY), F32)

    first = chunk * RUN
    total, rise, high_total, high_rise = one, own_below, one, own_above
    for t in range(RUN):
        down_ref[RUN - 1 - t] = high_total
        before = total
        total, rise = step(first + t, total, rise)
        pivot_ref[t] = before / total
        high_total, high_rise = step(first + RUN - 1 - t, high_total, high_rise)
    inverse = 1.0 / total
    close_ref[...] = 1.0 / (rise * inverse + pivot_ref[RUN - 1] * own_above)
    high_inverse = 1.0 / high_total
    for t in range(RUN):
        down_ref[t] = down_ref[t] * high_inverse


def forward_x_kernel(
    screening_ref, waves_ref, source_hbm, even_hbm, odd_hbm,
    out_ref, pivot_ref, down_ref, far_ref, close_ref, chunk_ref,
    source_ref, even_ref, odd_ref, shift_ref, column_ref, arrived,
):
    copies = [
        pltpu.make_async_copy(source_hbm, source_ref, arrived.at[0]),
        pltpu.make_async_copy(even_hbm, even_ref, arrived.at[1]),
        pltpu.make_async_copy(odd_hbm, odd_ref, arrived.at[2]),
    ]
    for copy in copies:
        copy.start()
    pivots(
        screening_ref, waves_ref, shift_ref, column_ref,
        pivot_ref, down_ref, far_ref, close_ref, chunk_ref,
    )
    for copy in copies:
        copy.wait()
    rows = source_ref[...].reshape(128, NX)
    low, high = rows[:, :HALF], rows[:, HALF:]
    out_ref[:HALF] = table_times_transposed(even_ref, low + high)
    out_ref[HALF:] = table_times_transposed(odd_ref, low - high)


def swap_halves(values):
    shape = values.shape
    return pltpu.roll(values.reshape(-1, 128), 64, 1).reshape(shape)


def lower_half(shape):
    return lax.broadcasted_iota(jnp.int32, shape, len(shape) - 1) < 64


def forward_y_kernel(chunk_ref, rows_ref, even_ref, odd_t_ref, pivot_ref, down_ref, modes_ref, send_ref):
    blocks = rows_ref[...].reshape(8, 8, LINES, 128)
    keep = lower_half((8, LINES, 128))

    def at(g):
        return blocks[G_IN.index(g)]

    def gather(parts):
        columns = []
        for pair in range(2):
            a, b = parts[2 * pair], parts[2 * pair + 1]
            first = jnp.where(keep, a, swap_halves(b))
            second = jnp.where(keep, swap_halves(a), b)
            columns.append(jnp.stack([first, second], axis=1).reshape(128, 128))
        return jnp.concatenate(columns, axis=1)

    sums = gather([at(g) + at(g + 4) for g in range(4)])
    differences = gather([at(g) - at(g + 4) for g in range(4)])
    modes_ref[:, :, :HALF] = times_table(sums, even_ref).reshape(RUN, LINES, HALF)
    modes_ref[:, :, HALF:] = times_table(differences, odd_t_ref).reshape(RUN, LINES, HALF)

    upward = jnp.zeros((LINES, NY), F32)
    downward = jnp.zeros((LINES, NY), F32)
    for t in range(RUN):
        plane = modes_ref[row(t, Y_IN)]
        upward = pivot_ref[t] * (plane + upward)
        downward = downward + down_ref[t] * plane
    chunk = chunk_ref[...]
    for other in range(CHUNKS):
        send_ref[RUN_ORDER.index(other)] = jnp.where(other > chunk, upward, downward)


def solve_kernel(chunk_ref, modes_ref, arrived_ref, pivot_ref, far_ref, close_ref, even_ref, odd_ref, out_ref, solved_ref):
    chunk = chunk_ref[...]
    below = jnp.zeros((LINES, NY), F32)
    above = jnp.zeros((LINES, NY), F32)
    for other in range(CHUNKS):
        below = jnp.where(other < chunk, arrived_ref[RUN_ORDER.index(other)] + far_ref[other] * below, below)
        rest = CHUNKS - 1 - other
        above = jnp.where(rest > chunk, arrived_ref[RUN_ORDER.index(rest)] + far_ref[rest] * above, above)

    elimination = below
    for t in range(RUN):
        elimination = pivot_ref[t] * (modes_ref[row(t, Y_IN)] + elimination)
        solved_ref[row(t, Y_OUT)] = elimination
    value = (elimination + pivot_ref[RUN - 1] * above) * close_ref[...]
    solved_ref[row(RUN - 1, Y_OUT)] = value
    for t in reversed(range(RUN - 1)):
        value = solved_ref[row(t, Y_OUT)] + pivot_ref[t] * value
        solved_ref[row(t, Y_OUT)] = value

    solved = solved_ref[...].reshape(128, NY)
    even = times_table(solved[:, :HALF], even_ref)
    odd = times_table(solved[:, HALF:], odd_ref)
    keep = lower_half((8, LINES, 128))
    for base, values in ((0, even + odd), (4, even - odd)):
        for pair in range(2):
            column = values[:, pair * 128 : pair * 128 + 128].reshape(8, 2, LINES, 128)
            a, b = column[:, 0], column[:, 1]
            out_ref[G_OUT.index(base + 2 * pair)] = jnp.where(keep, a, swap_halves(b))
            out_ref[G_OUT.index(base + 2 * pair + 1)] = jnp.where(keep, swap_halves(a), b)


def backward_x_kernel(rows_ref, even_ref, odd_ref, out_ref):
    blocks = rows_ref[...].reshape(8, 8, LINES, 128)
    ordered = [blocks[G_OUT.index(g), Y_OUT.index(y)] for g in G_IN for y in Y_IN]
    values = jnp.concatenate(ordered, axis=0).T
    even = times_table(values[:, :HALF], even_ref)
    odd = times_table(values[:, HALF:], odd_ref)
    scale = 1.0 / (NX * NY)
    out_ref[:, :, :HALF] = ((even + odd) * scale).reshape(2, 64, HALF)
    out_ref[:, :, HALF:] = ((even - odd) * scale).reshape(2, 64, HALF)


VMEM = pl.BlockSpec(memory_space=pltpu.VMEM)
HBM = pl.BlockSpec(memory_space=pltpu.HBM)
SMEM = pl.BlockSpec(memory_space=pltpu.SMEM)


def call(kernel, ins, outs, scratch=(), name=None, limit=16 * 1024 * 1024):
    return pl.pallas_call(
        kernel,
        in_specs=ins,
        out_specs=jax.tree.map(lambda _: VMEM, outs),
        out_shape=outs,
        scratch_shapes=list(scratch),
        compiler_params=pltpu.CompilerParams(vmem_limit_bytes=limit),
        name=name,
    )


def shape(*sizes):
    return jax.ShapeDtypeStruct(sizes, F32)


def run_peers(along_y, along_g):
    return [[run * PEERS + y * 8 + g for g in along_g for y in along_y] for run in range(CHUNKS)]


RUNS = [[run * 8 + y for run in RUN_ORDER] for y in range(8)]


def exchange_peers(values, along_y, along_g):
    pieces = values.reshape(PEERS, LINES, 128)
    pieces = lax.all_to_all(
        pieces, ("gz", "gy"), 0, 0, tiled=True, axis_index_groups=run_peers(along_y, along_g)
    )
    return pieces.reshape(512, 128)


def local(source, screening):
    even, odd, odd_t = (jnp.asarray(table) for table in half_tables())
    waves = wave_terms()
    planes = shape(RUN, LINES, NY)
    whole = jax.ShapeDtypeStruct((LINES, NY), jnp.int32)
    along_x, pivot, down, far, close, chunk = call(
        forward_x_kernel,
        [VMEM] * 2 + [HBM] * 3,
        (shape(512, 128), planes, planes, shape(CHUNKS, LINES, NY), shape(LINES, NY), whole),
        [
            pltpu.VMEM((2, 64, NX), F32),
            pltpu.VMEM((2 * HALF, HALF), BF16),
            pltpu.VMEM((2 * HALF, HALF), BF16),
            pltpu.VMEM((NZ, NZ), F32),
            pltpu.VMEM((128, 128), F32),
            pltpu.SemaphoreType.DMA((3,)),
        ],
        name="forward_x",
        limit=X_KERNEL_VMEM,
    )(screening[None, :], jnp.asarray(waves), source, even, odd)
    columns = exchange_peers(along_x, Y_IN, G_IN)
    modes, send = call(
        forward_y_kernel,
        [VMEM] * 6,
        (planes, shape(CHUNKS, LINES, NY)),
        name="forward_y",
    )(chunk, columns, even, odd_t, pivot, down)
    arrived = lax.all_to_all(send, "gz", 0, 0, tiled=True, axis_index_groups=RUNS)
    back_y = call(
        solve_kernel,
        [VMEM] * 8,
        shape(8, 8, LINES, 128),
        [pltpu.VMEM((RUN, LINES, NY), F32)],
        name="solve",
    )(chunk, modes, arrived, pivot, far, close, even, odd)
    rows = exchange_peers(back_y, Y_OUT, G_OUT)
    return call(backward_x_kernel, [VMEM] * 3, shape(2, 64, NX), name="backward_x")(
        rows, even, odd
    )


def solution(mesh):
    in_specs = (P("gz", "gy", None), P())
    out_specs = P("gz", "gy", None)
    return jax.shard_map(local, mesh=mesh, in_specs=in_specs, out_specs=out_specs, check_vma=False)
```

```python
import math

import jax
import jax.numpy as jnp
import ml_dtypes
import numpy as np
from jax import lax
from jax.experimental import pallas as pl
from jax.experimental.pallas import tpu as pltpu
from jax.sharding import PartitionSpec as P

NX = 512
NY = 512
NZ = 128
HALF = 256
CHUNKS = 8
RUN = NZ // CHUNKS
LINES = 8
PEERS = 64
RUN_ORDER = (4, 3, 5, 2, 6, 1, 7, 0)
Y_IN = (4, 5, 6, 7, 0, 1, 2, 3)
G_IN = (7, 0, 1, 2, 3, 4, 5, 6)
Y_OUT = (4, 5, 6, 7, 0, 1, 2, 3)
G_OUT = (5, 4, 7, 6, 1, 0, 3, 2)

X_KERNEL_VMEM = 55574528

F32 = jnp.float32
BF16 = jnp.bfloat16


def split_table(table):
    high = table.astype(ml_dtypes.bfloat16)
    low = (table - high.astype(np.float64)).astype(ml_dtypes.bfloat16)
    return np.concatenate([high, low], axis=0)


def cas(rows, columns, total):
    angle = (rows[:, None] * columns[None, :] % total) * (2.0 * math.pi / total)
    return np.cos(angle) + np.sin(angle)


def half_tables():
    index = np.arange(HALF)
    even = cas(2 * index, index, 2 * HALF)
    odd = cas(2 * index + 1, index, 2 * HALF)
    return split_table(even), split_table(odd), split_table(odd.T)


def wave_terms():
    index = np.concatenate([np.arange(0, 512, 2), np.arange(1, 512, 2)])
    return (4.0 * np.sin(index * (math.pi / 512)) ** 2).astype(np.float32).reshape(4, 128)


def split(values):
    high = values.astype(BF16)
    low = (values - high.astype(F32)).astype(BF16)
    return high, low


def times_table(values, table_ref):
    rows = values.shape[0]
    high, low = split(values)
    both = jnp.concatenate([high, low], axis=0)
    main = jnp.dot(both, table_ref[:HALF], preferred_element_type=F32)
    rest = jnp.dot(high, table_ref[HALF:], preferred_element_type=F32)
    return main[:rows] + (main[rows:] + rest)


def table_times_transposed(table_ref, values):
    rows = values.shape[0]
    high, low = split(values)
    both = jnp.concatenate([high, low], axis=0)
    product = lax.dot_general(
        table_ref[...], both, (((1,), (1,)), ((), ())), preferred_element_type=F32
    )
    return product[:HALF, :rows] + (product[:HALF, rows:] + product[HALF:, :rows])


def row(plane, order):
    return 2 * order.index(plane // 2) + plane % 2


def own_place():
    gz, gy = lax.axis_index("gz"), lax.axis_index("gy")
    return gz >> 3, (((gz & 7) + 8 - Y_IN[0]) & 7) * 8 + ((gy + 8 - G_IN[0]) & 7)


def pivots(screening_ref, waves_ref, shift_ref, column_ref, pivot_ref, down_ref, far_ref, close_ref, chunk_ref):
    chunk, group = own_place()
    chunk_ref[...] = jnp.zeros((LINES, NY), jnp.int32) + chunk
    shift_ref[...] = jnp.broadcast_to(screening_ref[...], (NZ, NZ)).T
    column_ref[...] = jnp.broadcast_to(waves_ref[pl.ds(group >> 4, 1), :], (128, 128)).T
    along_k = column_ref[pl.ds(pl.multiple_of((group & 15) * LINES, LINES), LINES), :]
    lam = jnp.concatenate([waves_ref[q : q + 1, :] + along_k for q in range(4)], axis=1)
    one = jnp.ones((LINES, NY), F32)

    def step(plane, total, rise):
        shift = shift_ref[pl.ds(plane, 1), :]
        rise = rise + (jnp.concatenate([shift] * 4, axis=1) + lam) * total
        return total + rise, rise

    below, above = one, one
    own_below, own_above = one, one
    for index in range(CHUNKS - 1):
        other = CHUNKS - 1 - index
        low_total, low_rise, high_total, high_rise = one, below, one, above
        for t in range(RUN):
            low_total, low_rise = step(index * RUN + t, low_total, low_rise)
            high_total, high_rise = step(other * RUN + RUN - 1 - t, high_total, high_rise)
        low_inverse, high_inverse = 1.0 / low_total, 1.0 / high_total

        @pl.when(index < chunk)
        def _():
            far_ref[index] = low_inverse

        @pl.when(other > chunk)
        def _():
            far_ref[other] = high_inverse

        below, above = low_rise * low_inverse, high_rise * high_inverse
        own_below = jnp.where(chunk == index + 1, below, own_below)
        own_above = jnp.where(chunk == other - 1, above, own_above)
    far_ref[chunk] = jnp.zeros((LINES, NY), F32)

    first = chunk * RUN
    total, rise, high_total, high_rise = one, own_below, one, own_above
    for t in range(RUN):
        down_ref[RUN - 1 - t] = high_total
        before = total
        total, rise = step(first + t, total, rise)
        pivot_ref[t] = before / total
        high_total, high_rise = step(first + RUN - 1 - t, high_total, high_rise)
    inverse = 1.0 / total
    close_ref[...] = 1.0 / (rise * inverse + pivot_ref[RUN - 1] * own_above)
    high_inverse = 1.0 / high_total
    for t in range(RUN):
        down_ref[t] = down_ref[t] * high_inverse


def forward_x_kernel(
    screening_ref, waves_ref, source_hbm, even_hbm, odd_hbm,
    out_ref, pivot_ref, down_ref, far_ref, close_ref, chunk_ref,
    source_ref, even_ref, odd_ref, shift_ref, column_ref, arrived,
):
    copies = [
        pltpu.make_async_copy(source_hbm, source_ref, arrived.at[0]),
        pltpu.make_async_copy(even_hbm, even_ref, arrived.at[1]),
        pltpu.make_async_copy(odd_hbm, odd_ref, arrived.at[2]),
    ]
    for copy in copies:
        copy.start()
    pivots(
        screening_ref, waves_ref, shift_ref, column_ref,
        pivot_ref, down_ref, far_ref, close_ref, chunk_ref,
    )
    for copy in copies:
        copy.wait()
    rows = source_ref[...].reshape(128, NX)
    low, high = rows[:, :HALF], rows[:, HALF:]
    out_ref[:HALF] = table_times_transposed(even_ref, low + high)
    out_ref[HALF:] = table_times_transposed(odd_ref, low - high)


def swap_halves(values):
    shape = values.shape
    return pltpu.roll(values.reshape(-1, 128), 64, 1).reshape(shape)


def lower_half(shape):
    return lax.broadcasted_iota(jnp.int32, shape, len(shape) - 1) < 64


def forward_y_kernel(chunk_ref, rows_ref, even_ref, odd_t_ref, pivot_ref, down_ref, modes_ref, send_ref):
    blocks = rows_ref[...].reshape(8, 8, LINES, 128)
    keep = lower_half((8, LINES, 128))

    def at(g):
        return blocks[:, G_IN.index(g)]

    def gather(parts):
        columns = []
        for pair in range(2):
            a, b = parts[2 * pair], parts[2 * pair + 1]
            first = jnp.where(keep, a, swap_halves(b))
            second = jnp.where(keep, swap_halves(a), b)
            columns.append(jnp.stack([first, second], axis=1).reshape(128, 128))
        return jnp.concatenate(columns, axis=1)

    sums = gather([at(g) + at(g + 4) for g in range(4)])
    differences = gather([at(g) - at(g + 4) for g in range(4)])
    modes_ref[:, :, :HALF] = times_table(sums, even_ref).reshape(RUN, LINES, HALF)
    modes_ref[:, :, HALF:] = times_table(differences, odd_t_ref).reshape(RUN, LINES, HALF)

    upward = jnp.zeros((LINES, NY), F32)
    downward = jnp.zeros((LINES, NY), F32)
    for t in range(RUN):
        plane = modes_ref[row(t, Y_IN)]
        upward = pivot_ref[t] * (plane + upward)
        modes_ref[row(t, Y_IN)] = upward
        downward = downward + down_ref[t] * plane
    chunk = chunk_ref[...]
    for other in range(CHUNKS):
        send_ref[RUN_ORDER.index(other)] = jnp.where(other > chunk, upward, downward)


def solve_kernel(chunk_ref, modes_ref, arrived_ref, pivot_ref, far_ref, close_ref, even_ref, odd_ref, out_ref, solved_ref):
    chunk = chunk_ref[...]
    below = jnp.zeros((LINES, NY), F32)
    above = jnp.zeros((LINES, NY), F32)
    for other in range(CHUNKS):
        below = jnp.where(other < chunk, arrived_ref[RUN_ORDER.index(other)] + far_ref[other] * below, below)
        rest = CHUNKS - 1 - other
        above = jnp.where(rest > chunk, arrived_ref[RUN_ORDER.index(rest)] + far_ref[rest] * above, above)

    carried = below
    for t in range(RUN):
        carried = pivot_ref[t] * carried
        elimination = modes_ref[row(t, Y_IN)] + carried
        solved_ref[row(t, Y_OUT)] = elimination
    value = (elimination + pivot_ref[RUN - 1] * above) * close_ref[...]
    solved_ref[row(RUN - 1, Y_OUT)] = value
    for t in reversed(range(RUN - 1)):
        value = solved_ref[row(t, Y_OUT)] + pivot_ref[t] * value
        solved_ref[row(t, Y_OUT)] = value

    solved = solved_ref[...].reshape(128, NY)
    even = times_table(solved[:, :HALF], even_ref)
    odd = times_table(solved[:, HALF:], odd_ref)
    keep = lower_half((8, LINES, 128))
    for base, values in ((0, even + odd), (4, even - odd)):
        for pair in range(2):
            column = values[:, pair * 128 : pair * 128 + 128].reshape(8, 2, LINES, 128)
            a, b = column[:, 0], column[:, 1]
            out_ref[:, G_OUT.index(base + 2 * pair)] = jnp.where(keep, a, swap_halves(b))
            out_ref[:, G_OUT.index(base + 2 * pair + 1)] = jnp.where(keep, swap_halves(a), b)


def backward_x_kernel(rows_ref, even_ref, odd_ref, out_ref):
    blocks = rows_ref[...].reshape(8, 8, LINES, 128)
    ordered = [blocks[Y_OUT.index(y), G_OUT.index(g)] for y in Y_IN for g in G_IN]
    values = jnp.concatenate(ordered, axis=0).T
    even = times_table(values[:, :HALF], even_ref)
    odd = times_table(values[:, HALF:], odd_ref)
    scale = 1.0 / (NX * NY)
    out_ref[:, :, :HALF] = ((even + odd) * scale).reshape(2, 64, HALF)
    out_ref[:, :, HALF:] = ((even - odd) * scale).reshape(2, 64, HALF)


VMEM = pl.BlockSpec(memory_space=pltpu.VMEM)
HBM = pl.BlockSpec(memory_space=pltpu.HBM)
SMEM = pl.BlockSpec(memory_space=pltpu.SMEM)


def call(kernel, ins, outs, scratch=(), name=None, limit=16 * 1024 * 1024):
    return pl.pallas_call(
        kernel,
        in_specs=ins,
        out_specs=jax.tree.map(lambda _: VMEM, outs),
        out_shape=outs,
        scratch_shapes=list(scratch),
        compiler_params=pltpu.CompilerParams(vmem_limit_bytes=limit),
        name=name,
    )


def shape(*sizes):
    return jax.ShapeDtypeStruct(sizes, F32)


def run_peers(along_y, along_g):
    return [[run * PEERS + y * 8 + g for y in along_y for g in along_g] for run in range(CHUNKS)]


RUNS = [[run * 8 + y for run in RUN_ORDER] for y in range(8)]


def exchange_peers(values, along_y, along_g):
    pieces = values.reshape(PEERS, LINES, 128)
    pieces = lax.all_to_all(
        pieces, ("gz", "gy"), 0, 0, tiled=True, axis_index_groups=run_peers(along_y, along_g)
    )
    return pieces.reshape(512, 128)


def local(source, screening):
    even, odd, odd_t = (jnp.asarray(table) for table in half_tables())
    waves = wave_terms()
    planes = shape(RUN, LINES, NY)
    whole = jax.ShapeDtypeStruct((LINES, NY), jnp.int32)
    along_x, pivot, down, far, close, chunk = call(
        forward_x_kernel,
        [VMEM] * 2 + [HBM] * 3,
        (shape(512, 128), planes, planes, shape(CHUNKS, LINES, NY), shape(LINES, NY), whole),
        [
            pltpu.VMEM((2, 64, NX), F32),
            pltpu.VMEM((2 * HALF, HALF), BF16),
            pltpu.VMEM((2 * HALF, HALF), BF16),
            pltpu.VMEM((NZ, NZ), F32),
            pltpu.VMEM((128, 128), F32),
            pltpu.SemaphoreType.DMA((3,)),
        ],
        name="forward_x",
        limit=X_KERNEL_VMEM,
    )(screening[None, :], jnp.asarray(waves), source, even, odd)
    columns = exchange_peers(along_x, Y_IN, G_IN)
    modes, send = call(
        forward_y_kernel,
        [VMEM] * 6,
        (planes, shape(CHUNKS, LINES, NY)),
        name="forward_y",
    )(chunk, columns, even, odd_t, pivot, down)
    arrived = lax.all_to_all(send, "gz", 0, 0, tiled=True, axis_index_groups=RUNS)
    back_y = call(
        solve_kernel,
        [VMEM] * 8,
        shape(8, 8, LINES, 128),
        [pltpu.VMEM((RUN, LINES, NY), F32)],
        name="solve",
    )(chunk, modes, arrived, pivot, far, close, even, odd)
    rows = exchange_peers(back_y, Y_OUT, G_OUT)
    return call(backward_x_kernel, [VMEM] * 3, shape(2, 64, NX), name="backward_x")(
        rows, even, odd
    )


def solution(mesh):
    in_specs = (P("gz", "gy", None), P())
    out_specs = P("gz", "gy", None)
    return jax.shard_map(local, mesh=mesh, in_specs=in_specs, out_specs=out_specs, check_vma=False)
```

```python
import math

import jax
import jax.numpy as jnp
import ml_dtypes
import numpy as np
from jax import lax
from jax.experimental import pallas as pl
from jax.experimental.pallas import tpu as pltpu
from jax.sharding import PartitionSpec as P

NX = 512
NY = 512
NZ = 128
HALF = 256
CHUNKS = 8
RUN = NZ // CHUNKS
LINES = 8
PEERS = 64
RUN_ORDER = (4, 3, 5, 2, 6, 1, 7, 0)
Y_IN = (4, 5, 6, 7, 0, 1, 2, 3)
G_IN = (5, 6, 7, 0, 1, 2, 3, 4)
Y_OUT = (4, 5, 6, 7, 0, 1, 2, 3)
G_OUT = (5, 4, 7, 6, 1, 0, 3, 2)

X_KERNEL_VMEM = 55574528

F32 = jnp.float32
BF16 = jnp.bfloat16


def split_table(table):
    high = table.astype(ml_dtypes.bfloat16)
    low = (table - high.astype(np.float64)).astype(ml_dtypes.bfloat16)
    return np.concatenate([high, low], axis=0)


def cas(rows, columns, total):
    angle = (rows[:, None] * columns[None, :] % total) * (2.0 * math.pi / total)
    return np.cos(angle) + np.sin(angle)


def half_tables():
    index = np.arange(HALF)
    even = cas(2 * index, index, 2 * HALF)
    odd = cas(2 * index + 1, index, 2 * HALF)
    return split_table(even), split_table(odd), split_table(odd.T)


def wave_terms():
    index = np.concatenate([np.arange(0, 512, 2), np.arange(1, 512, 2)])
    return (4.0 * np.sin(index * (math.pi / 512)) ** 2).astype(np.float32).reshape(4, 128)


def split(values):
    high = values.astype(BF16)
    low = (values - high.astype(F32)).astype(BF16)
    return high, low


def times_table(values, table_ref):
    rows = values.shape[0]
    high, low = split(values)
    both = jnp.concatenate([high, low], axis=0)
    main = jnp.dot(both, table_ref[:HALF], preferred_element_type=F32)
    rest = jnp.dot(high, table_ref[HALF:], preferred_element_type=F32)
    return main[:rows] + (main[rows:] + rest)


def table_times_transposed(table_ref, values):
    rows = values.shape[0]
    high, low = split(values)
    both = jnp.concatenate([high, low], axis=0)
    product = lax.dot_general(
        table_ref[...], both, (((1,), (1,)), ((), ())), preferred_element_type=F32
    )
    return product[:HALF, :rows] + (product[:HALF, rows:] + product[HALF:, :rows])


def row(plane, order):
    return 2 * order.index(plane // 2) + plane % 2


def own_place():
    gz, gy = lax.axis_index("gz"), lax.axis_index("gy")
    return gz >> 3, (((gz & 7) + 8 - Y_IN[0]) & 7) * 8 + ((gy + 8 - G_IN[0]) & 7)


def pivots(screening_ref, waves_ref, shift_ref, column_ref, pivot_ref, down_ref, far_ref, close_ref, chunk_ref):
    chunk, group = own_place()
    chunk_ref[...] = jnp.zeros((LINES, NY), jnp.int32) + chunk
    shift_ref[...] = jnp.broadcast_to(screening_ref[...], (NZ, NZ)).T
    column_ref[...] = jnp.broadcast_to(waves_ref[pl.ds(group >> 4, 1), :], (128, 128)).T
    along_k = column_ref[pl.ds(pl.multiple_of((group & 15) * LINES, LINES), LINES), :]
    lam = jnp.concatenate([waves_ref[q : q + 1, :] + along_k for q in range(4)], axis=1)
    one = jnp.ones((LINES, NY), F32)

    def step(plane, total, rise):
        shift = shift_ref[pl.ds(plane, 1), :]
        rise = rise + (jnp.concatenate([shift] * 4, axis=1) + lam) * total
        return total + rise, rise

    below, above = one, one
    own_below, own_above = one, one
    for index in range(CHUNKS - 1):
        other = CHUNKS - 1 - index
        low_total, low_rise, high_total, high_rise = one, below, one, above
        for t in range(RUN):
            low_total, low_rise = step(index * RUN + t, low_total, low_rise)
            high_total, high_rise = step(other * RUN + RUN - 1 - t, high_total, high_rise)
        low_inverse, high_inverse = 1.0 / low_total, 1.0 / high_total

        @pl.when(index < chunk)
        def _():
            far_ref[index] = low_inverse

        @pl.when(other > chunk)
        def _():
            far_ref[other] = high_inverse

        below, above = low_rise * low_inverse, high_rise * high_inverse
        own_below = jnp.where(chunk == index + 1, below, own_below)
        own_above = jnp.where(chunk == other - 1, above, own_above)
    far_ref[chunk] = jnp.zeros((LINES, NY), F32)

    first = chunk * RUN
    total, rise, high_total, high_rise = one, own_below, one, own_above
    for t in range(RUN):
        down_ref[RUN - 1 - t] = high_total
        before = total
        total, rise = step(first + t, total, rise)
        pivot_ref[t] = before / total
        high_total, high_rise = step(first + RUN - 1 - t, high_total, high_rise)
    inverse = 1.0 / total
    close_ref[...] = 1.0 / (rise * inverse + pivot_ref[RUN - 1] * own_above)
    high_inverse = 1.0 / high_total
    for t in range(RUN):
        down_ref[t] = down_ref[t] * high_inverse


def forward_x_kernel(
    screening_ref, waves_ref, source_hbm, even_hbm, odd_hbm,
    out_ref, pivot_ref, down_ref, far_ref, close_ref, chunk_ref,
    source_ref, even_ref, odd_ref, shift_ref, column_ref, arrived,
):
    copies = [
        pltpu.make_async_copy(source_hbm, source_ref, arrived.at[0]),
        pltpu.make_async_copy(even_hbm, even_ref, arrived.at[1]),
        pltpu.make_async_copy(odd_hbm, odd_ref, arrived.at[2]),
    ]
    for copy in copies:
        copy.start()
    pivots(
        screening_ref, waves_ref, shift_ref, column_ref,
        pivot_ref, down_ref, far_ref, close_ref, chunk_ref,
    )
    for copy in copies:
        copy.wait()
    rows = source_ref[...].reshape(128, NX)
    low, high = rows[:, :HALF], rows[:, HALF:]
    out_ref[:HALF] = table_times_transposed(even_ref, low + high)
    out_ref[HALF:] = table_times_transposed(odd_ref, low - high)


def swap_halves(values):
    shape = values.shape
    return pltpu.roll(values.reshape(-1, 128), 64, 1).reshape(shape)


def lower_half(shape):
    return lax.broadcasted_iota(jnp.int32, shape, len(shape) - 1) < 64


def forward_y_kernel(chunk_ref, rows_ref, even_ref, odd_t_ref, pivot_ref, down_ref, modes_ref, send_ref):
    blocks = rows_ref[...].reshape(8, 8, LINES, 128)
    keep = lower_half((8, LINES, 128))

    def at(g):
        return blocks[:, G_IN.index(g)]

    def gather(parts):
        columns = []
        for pair in range(2):
            a, b = parts[2 * pair], parts[2 * pair + 1]
            first = jnp.where(keep, a, swap_halves(b))
            second = jnp.where(keep, swap_halves(a), b)
            columns.append(jnp.stack([first, second], axis=1).reshape(128, 128))
        return jnp.concatenate(columns, axis=1)

    sums = gather([at(g) + at(g + 4) for g in range(4)])
    differences = gather([at(g) - at(g + 4) for g in range(4)])
    modes_ref[:, :, :HALF] = times_table(sums, even_ref).reshape(RUN, LINES, HALF)
    modes_ref[:, :, HALF:] = times_table(differences, odd_t_ref).reshape(RUN, LINES, HALF)

    upward = jnp.zeros((LINES, NY), F32)
    downward = jnp.zeros((LINES, NY), F32)
    for t in range(RUN):
        plane = modes_ref[row(t, Y_IN)]
        upward = pivot_ref[t] * (plane + upward)
        modes_ref[row(t, Y_IN)] = upward
        downward = downward + down_ref[t] * plane
    chunk = chunk_ref[...]
    for other in range(CHUNKS):
        send_ref[RUN_ORDER.index(other)] = jnp.where(other > chunk, upward, downward)


def solve_kernel(chunk_ref, modes_ref, arrived_ref, pivot_ref, far_ref, close_ref, even_ref, odd_ref, out_ref, solved_ref):
    chunk = chunk_ref[...]
    below = jnp.zeros((LINES, NY), F32)
    above = jnp.zeros((LINES, NY), F32)
    for other in range(CHUNKS):
        below = jnp.where(other < chunk, arrived_ref[RUN_ORDER.index(other)] + far_ref[other] * below, below)
        rest = CHUNKS - 1 - other
        above = jnp.where(rest > chunk, arrived_ref[RUN_ORDER.index(rest)] + far_ref[rest] * above, above)

    carried = below
    for t in range(RUN):
        carried = pivot_ref[t] * carried
        elimination = modes_ref[row(t, Y_IN)] + carried
        solved_ref[row(t, Y_OUT)] = elimination
    value = (elimination + pivot_ref[RUN - 1] * above) * close_ref[...]
    solved_ref[row(RUN - 1, Y_OUT)] = value
    for t in reversed(range(RUN - 1)):
        value = solved_ref[row(t, Y_OUT)] + pivot_ref[t] * value
        solved_ref[row(t, Y_OUT)] = value

    solved = solved_ref[...].reshape(128, NY)
    even = times_table(solved[:, :HALF], even_ref)
    odd = times_table(solved[:, HALF:], odd_ref)
    keep = lower_half((8, LINES, 128))
    for base, values in ((0, even + odd), (4, even - odd)):
        for pair in range(2):
            column = values[:, pair * 128 : pair * 128 + 128].reshape(8, 2, LINES, 128)
            a, b = column[:, 0], column[:, 1]
            out_ref[:, G_OUT.index(base + 2 * pair)] = jnp.where(keep, a, swap_halves(b))
            out_ref[:, G_OUT.index(base + 2 * pair + 1)] = jnp.where(keep, swap_halves(a), b)


def backward_x_kernel(rows_ref, even_ref, odd_ref, out_ref):
    blocks = rows_ref[...].reshape(8, 8, LINES, 128)
    ordered = [blocks[Y_OUT.index(y), G_OUT.index(g)] for y in Y_IN for g in G_IN]
    values = jnp.concatenate(ordered, axis=0).T
    even = times_table(values[:, :HALF], even_ref)
    odd = times_table(values[:, HALF:], odd_ref)
    scale = 1.0 / (NX * NY)
    out_ref[:, :, :HALF] = ((even + odd) * scale).reshape(2, 64, HALF)
    out_ref[:, :, HALF:] = ((even - odd) * scale).reshape(2, 64, HALF)


VMEM = pl.BlockSpec(memory_space=pltpu.VMEM)
HBM = pl.BlockSpec(memory_space=pltpu.HBM)
SMEM = pl.BlockSpec(memory_space=pltpu.SMEM)


def call(kernel, ins, outs, scratch=(), name=None, limit=16 * 1024 * 1024):
    return pl.pallas_call(
        kernel,
        in_specs=ins,
        out_specs=jax.tree.map(lambda _: VMEM, outs),
        out_shape=outs,
        scratch_shapes=list(scratch),
        compiler_params=pltpu.CompilerParams(vmem_limit_bytes=limit),
        name=name,
    )


def shape(*sizes):
    return jax.ShapeDtypeStruct(sizes, F32)


def run_peers(along_y, along_g):
    return [[run * PEERS + y * 8 + g for y in along_y for g in along_g] for run in range(CHUNKS)]


RUNS = [[run * 8 + y for run in RUN_ORDER] for y in range(8)]


def exchange_peers(values, along_y, along_g):
    pieces = values.reshape(PEERS, LINES, 128)
    pieces = lax.all_to_all(
        pieces, ("gz", "gy"), 0, 0, tiled=True, axis_index_groups=run_peers(along_y, along_g)
    )
    return pieces.reshape(512, 128)


def local(source, screening):
    even, odd, odd_t = (jnp.asarray(table) for table in half_tables())
    waves = wave_terms()
    planes = shape(RUN, LINES, NY)
    whole = jax.ShapeDtypeStruct((LINES, NY), jnp.int32)
    along_x, pivot, down, far, close, chunk = call(
        forward_x_kernel,
        [VMEM] * 2 + [HBM] * 3,
        (shape(512, 128), planes, planes, shape(CHUNKS, LINES, NY), shape(LINES, NY), whole),
        [
            pltpu.VMEM((2, 64, NX), F32),
            pltpu.VMEM((2 * HALF, HALF), BF16),
            pltpu.VMEM((2 * HALF, HALF), BF16),
            pltpu.VMEM((NZ, NZ), F32),
            pltpu.VMEM((128, 128), F32),
            pltpu.SemaphoreType.DMA((3,)),
        ],
        name="forward_x",
        limit=X_KERNEL_VMEM,
    )(screening[None, :], jnp.asarray(waves), source, even, odd)
    columns = exchange_peers(along_x, Y_IN, G_IN)
    modes, send = call(
        forward_y_kernel,
        [VMEM] * 6,
        (planes, shape(CHUNKS, LINES, NY)),
        name="forward_y",
    )(chunk, columns, even, odd_t, pivot, down)
    arrived = lax.all_to_all(send, "gz", 0, 0, tiled=True, axis_index_groups=RUNS)
    back_y = call(
        solve_kernel,
        [VMEM] * 8,
        shape(8, 8, LINES, 128),
        [pltpu.VMEM((RUN, LINES, NY), F32)],
        name="solve",
    )(chunk, modes, arrived, pivot, far, close, even, odd)
    rows = exchange_peers(back_y, Y_OUT, G_OUT)
    return call(backward_x_kernel, [VMEM] * 3, shape(2, 64, NX), name="backward_x")(
        rows, even, odd
    )


def solution(mesh):
    in_specs = (P("gz", "gy", None), P())
    out_specs = P("gz", "gy", None)
    return jax.shard_map(local, mesh=mesh, in_specs=in_specs, out_specs=out_specs, check_vma=False)
```
